32 devices in a mesh: groups: 2 (over y), wide: 4 (over z), narrow: 4 (over x, core).
Axes of the slice: x: 2, y: 2, z: 4, core: 2. Of those that a mesh axis runs over, the one named last changes fastest.
Arguments:
- hidden: bfloat16 [16, 16384], P(('groups', 'narrow'), 'wide'), parts along dimension 0, may hold values from -6 to 6
- lengths: int32 [16], P(('groups', 'wide')), parts along dimension 0, may hold values from 1 to 2048, 8192 in all
- w_query: bfloat16 [16384, 16384], P('wide', 'narrow'), may hold values from -0.046875 to 0.046875
- key_weight: bfloat16 [16384, 1024], P('wide', 'narrow'), may hold values from -0.046875 to 0.046875
- value_weight: bfloat16 [16384, 1024], P('wide', 'narrow'), may hold values from -0.046875 to 0.046875
- w_out: bfloat16 [16384, 16384], P('narrow', 'wide'), may hold values from -0.046875 to 0.046875
- key_cache: bfloat16 [16, 8, 2048, 128], P(('groups', 'wide'), 'narrow'), parts along dimension 0, may hold values from -204 to 204
- cached_values: bfloat16 [16, 8, 2048, 128], P(('groups', 'wide'), 'narrow'), parts along dimension 0, may hold values from -6 to 6
Outputs:
- attended: bfloat16 [16, 16384], P(('groups', 'narrow'), 'wide'), parts along dimension 0
The draws below stay inside these ranges and needn't reach their ends.
There are 2 independent parts, one for each index of `groups`. The reference program is written for one: setup_inputs(seed, part) draws one part's arguments, and reference() takes and returns one part's arrays. A program takes and returns all parts, laid end to end along the dimension named above; an argument that names none is the same for every part. Nothing has to cross between parts.
Inputs may be any that keep to these rules, and one draw needn't show every extreme that they name: Row r's cache holds valid entries at its first lengths[r] positions; the largest length equals 2048 in every draw.
All inputs are finite; a program needn't handle non-finite values. No bound on the sum of `lengths` on one device may be relied on, other than what follows from the above.
Results may differ from the reference program's by a relative error of at most 0.018.
Values may be sent and summed in bfloat16 or wider, within the bound.
No kernel may reach another device: no remote copies, remote signals or barrier semaphores. Data moves between devices by JAX's collectives and lax.ppermute only.
A program may use at most 192 MiB of HBM per device.

```python
import math
import jax
import jax.numpy as jnp
import numpy as np
from jax import lax

MODEL_WIDTH = 16384
QUERY_HEADS = 128
KEY_VALUE_HEADS = 8
HEAD_SIZE = 128
CACHE_SLOTS = 2048
ROWS_OVERALL = 8


def draw_key_cache(key, part):
    key = jax.random.fold_in(key, 11)
    key_one = jax.random.fold_in(key, 0)
    array_dims = (ROWS_OVERALL, KEY_VALUE_HEADS, CACHE_SLOTS, HEAD_SIZE)
    entries = jnp.clip(jax.random.normal(key_one, array_dims, jnp.float32), -6.0, 6.0)
    return entries.astype(jnp.bfloat16)


def strengthened(result, key, source, target, shards_of, factor):
    owner, partner = [(jnp.arange(result.shape[axis_at]) // (result.shape[axis_at] // shards_of)).reshape([-1 if axis == axis_at else 1 for axis in range(result.ndim)]) for axis_at in (source, target)]
    chosen = jax.random.permutation(key, shards_of)[partner]
    strong = (owner == chosen) | (owner == (partner + shards_of // 2) % shards_of)
    return jnp.where(strong, factor * result, result)


def steps_of(key, dims, shards, low, high):
    def one(dim, blocks):
        draws = jax.random.uniform(jax.random.fold_in(jax.random.fold_in(key, 6), dim), (blocks,), jnp.float32, low / len(shards), high / len(shards))
        return jnp.repeat(jnp.exp(draws), dims[dim] // blocks).reshape((-1,) + (1,) * (len(dims) - dim - 1))

    gain = one(*shards[0])
    for cut in shards[1:]:
        gain = gain * one(*cut)
    return gain


def length_profile(count, total, most, skew):
    loads = [(1 << 20) // math.isqrt(rank ** skew) + 1 for rank in range(2, count + 1)]
    surplus, holding = total - most - (count - 1), [1] * (count - 1)
    while surplus > 0:
        movable = [i for i in range(count - 1) if holding[i] < most]
        whole, left = sum([loads[i] for i in movable]), surplus
        for i in movable:
            extra = min(most - holding[i], max(1, left * loads[i] // whole), surplus)
            holding[i] = holding[i] + extra
            surplus = surplus - extra
    return np.array([most] + holding)


def uneven(stream_key, number_of, total, reach, slope):
    if number_of == 2:
        one = jax.random.randint(stream_key, (), max(1, total - reach), min(reach, total - 1) + 1)
        return jnp.stack([one, total - one])
    sizes = jnp.asarray(length_profile(number_of, total, reach, slope), jnp.int32)
    couples = (number_of - 1) // 2
    source_of, taker = sizes[1:1 + 2 * couples:2], sizes[2:2 + 2 * couples:2]
    slack = jnp.minimum(source_of - 1, reach - taker)
    passed = jax.random.randint(jax.random.fold_in(stream_key, 1), (couples,), 0, 1 << 20) % (slack + 1)
    sizes = sizes.at[1:1 + 2 * couples:2].set(source_of - passed).at[2:2 + 2 * couples:2].set(taker + passed)
    return sizes[jax.random.permutation(jax.random.fold_in(stream_key, 2), number_of)]


def centred(rng, shape, scale, limit, cuts=(), held_as=jnp.bfloat16):
    drawn = scale * jax.random.normal(rng, shape, jnp.float32)
    if cuts:
        drawn = drawn * steps_of(rng, shape, cuts, -0.22, 0.18)
    return jnp.clip(drawn, -limit, limit).astype(held_as)


def gaussian_with(stream_key, extent, spread, limit, cuts, heavy, held_as=jnp.bfloat16):
    values = spread * jax.random.normal(stream_key, extent, jnp.float32)
    if cuts:
        values = values * steps_of(stream_key, extent, cuts, -0.22, 0.18)
    return jnp.clip(strengthened(values, jax.random.fold_in(stream_key, 3), *heavy), -limit, limit).astype(held_as)


def setup_inputs(seed: int = 0, part: int = 0) -> dict:
    streams_of = jax.random.split(jax.random.key(seed), 9)
    part_keys = jax.random.split(jax.random.fold_in(streams_of[8], part), 9)
    return {
        "hidden": gaussian_with(part_keys[0], (ROWS_OVERALL, MODEL_WIDTH), 1.0, 6.0, ((0, 4), (1, 4)), (1, 0, 4, 2.0)),
        "lengths": uneven(part_keys[1], ROWS_OVERALL, ROWS_OVERALL * CACHE_SLOTS // 2, CACHE_SLOTS, 2).astype(jnp.int32),
        "w_query": centred(streams_of[2], (MODEL_WIDTH, QUERY_HEADS * HEAD_SIZE), MODEL_WIDTH ** -0.5, 0.046875, ((0, 4), (1, 4))),
        "key_weight": centred(streams_of[3], (MODEL_WIDTH, KEY_VALUE_HEADS * HEAD_SIZE), MODEL_WIDTH ** -0.5, 0.046875, ((0, 4), (1, 4))),
        "value_weight": centred(streams_of[4], (MODEL_WIDTH, KEY_VALUE_HEADS * HEAD_SIZE), MODEL_WIDTH ** -0.5, 0.046875, ((0, 4), (1, 4))),
        "w_out": centred(streams_of[5], (QUERY_HEADS * HEAD_SIZE, MODEL_WIDTH), (QUERY_HEADS * HEAD_SIZE) ** -0.5, 0.046875, ((0, 4), (1, 4))),
        "key_cache": draw_key_cache(jax.random.fold_in(jax.random.fold_in(streams_of[8], part), 71), part),
        "cached_values": centred(part_keys[7], (ROWS_OVERALL, KEY_VALUE_HEADS, CACHE_SLOTS, HEAD_SIZE), 1.0, 6.0, ((0, 4), (1, 4))),
    }


def rotary(vectors, positions):
    head_dim = vectors.shape[-1]
    half_dim = head_dim // 2
    exponents = jnp.arange(half_dim, dtype=jnp.float32) * (2.0 / head_dim)
    frequency = jnp.exp(-math.log(500000.0) * exponents)
    angles = positions.astype(jnp.float32)[:, None] * frequency[None, :]
    cos_part = jnp.cos(angles)[:, None, :]
    sin_part = jnp.sin(angles)[:, None, :]
    front_half = vectors[..., :half_dim]
    back_half = vectors[..., half_dim:]
    return jnp.concatenate([front_half * cos_part - back_half * sin_part, back_half * cos_part + front_half * sin_part], -1)


def attend_row(inputs):
    row_query, key_row, value_row, keys_row, values_row, length_row = inputs
    heads_per_group = QUERY_HEADS // KEY_VALUE_HEADS
    score_scale = HEAD_SIZE ** -0.5
    grouped_query = row_query.reshape(KEY_VALUE_HEADS, heads_per_group, HEAD_SIZE).astype(jnp.float32)
    scores = jnp.einsum('hgd,hld->hgl', grouped_query, keys_row.astype(jnp.float32)) * score_scale
    self_score = jnp.einsum('hgd,hd->hg', grouped_query, key_row.astype(jnp.float32)) * score_scale
    inside = (jnp.arange(CACHE_SLOTS) < length_row)[None, None, :]
    masked = jnp.where(inside, scores, -jnp.inf)
    highest = jnp.maximum(jnp.max(masked, -1), self_score)
    weights = jnp.where(inside, jnp.exp(scores - highest[..., None]), 0.0)
    self_weight = jnp.exp(self_score - highest)
    denominator = jnp.sum(weights, -1) + self_weight
    mixed = jnp.einsum('hgl,hld->hgd', weights.astype(jnp.bfloat16).astype(jnp.float32), values_row.astype(jnp.float32))
    mixed = mixed + self_weight.astype(jnp.bfloat16).astype(jnp.float32)[..., None] * value_row.astype(jnp.float32)[:, None, :]
    return (mixed / denominator[..., None]).astype(jnp.bfloat16).reshape(QUERY_HEADS * HEAD_SIZE)


def reference(hidden, lengths, w_query, key_weight, value_weight, w_out, key_cache, cached_values):
    query = jnp.dot(hidden, w_query, preferred_element_type=jnp.float32).reshape(ROWS_OVERALL, QUERY_HEADS, HEAD_SIZE)
    fresh_key = jnp.dot(hidden, key_weight, preferred_element_type=jnp.float32).reshape(ROWS_OVERALL, KEY_VALUE_HEADS, HEAD_SIZE)
    fresh_value = jnp.dot(hidden, value_weight, preferred_element_type=jnp.float32).astype(jnp.bfloat16).reshape(ROWS_OVERALL, KEY_VALUE_HEADS, HEAD_SIZE)
    query_rot = rotary(query, lengths).astype(jnp.bfloat16)
    key_rot = rotary(fresh_key, lengths).astype(jnp.bfloat16)
    context = lax.map(attend_row, (query_rot, key_rot, fresh_value, key_cache, cached_values, lengths))
    return jnp.dot(context, w_out, preferred_element_type=jnp.float32).astype(jnp.bfloat16)
```

```python
import functools
import math

import jax
import jax.numpy as jnp
from jax import lax
from jax.experimental import pallas as pl
from jax.experimental.pallas import tpu as pltpu
from jax.sharding import PartitionSpec as P

MIB = 1 << 20
LANES = 128
THETA = 500000.0
DIRECT_PEERS = 8


def xor_pairs(count, step):
    return [(i, i ^ step) for i in range(count)]


def direct(count):
    return count <= DIRECT_PEERS and count & (count - 1) == 0


def gather_pieces(piece, axis, count):
    if direct(count):
        return [piece] + [lax.ppermute(piece, axis, xor_pairs(count, t)) for t in range(1, count)]
    whole = lax.all_gather(piece, axis, axis=0, tiled=False)
    return [whole[t] for t in range(count)]


def scatter_pieces(pieces, axis, count):
    if direct(count):
        return [pieces[0]] + [
            lax.ppermute(pieces[t], axis, xor_pairs(count, t)) for t in range(1, count)
        ]
    return [lax.psum_scatter(jnp.stack(pieces), axis, scatter_dimension=0, tiled=False)]


def peer(me, t, count):
    return me ^ t if direct(count) else t


def vmem():
    return pl.BlockSpec(memory_space=pltpu.VMEM)


def smem():
    return pl.BlockSpec(memory_space=pltpu.SMEM)


def project_kernel(
    places, w_query, key_weight, value_weight, *refs, pieces, heads, kv, stride, depth, slots
):
    inputs, refs = refs[:pieces], refs[pieces:]
    outs, (rows, total, laid, held, sems) = refs[:-5], refs[-5:]
    width, columns = w_query.shape
    chunks = width // depth

    def copy(i):
        return pltpu.make_async_copy(
            w_query.at[pl.ds(i * depth, depth)], held.at[i % slots], sems.at[i % slots]
        )

    for i in range(min(slots, chunks)):
        copy(i).start()
    rows[...] = jnp.concatenate([p[...].astype(jnp.float32) for p in inputs], 0).astype(
        jnp.bfloat16
    )
    count = rows.shape[0]
    group = min(8, count)
    fresh = [
        jnp.dot(rows[...], w[...], preferred_element_type=jnp.float32)
        for w in (key_weight, value_weight)
    ]
    for i in range(chunks):
        copy(i).wait()
        term = jnp.dot(
            rows[:, i * depth : (i + 1) * depth],
            held[i % slots],
            preferred_element_type=jnp.float32,
        )
        total[...] = term if i == 0 else total[...] + term
        if i + slots < chunks:
            copy(i + slots).start()
    for base in range(0, count, group):
        for h in range(heads + 2 * kv):
            if h < heads:
                block = total[base : base + group, h * LANES : (h + 1) * LANES]
            else:
                which, j = divmod(h - heads, kv)
                block = fresh[which][base : base + group, j * LANES : (j + 1) * LANES]
            laid[pl.ds(base * stride + h, group, stride=stride), :] = block
    for t, out in enumerate(outs):
        out[...] = laid[pl.ds(pl.multiple_of(places[t] * stride, 8), out.shape[0]), :]


def project(places, hidden_pieces, w_query, key_weight, value_weight, row_count, heads, kv):
    stride = -(-(heads + 2 * kv) // 8) * 8
    width, columns = w_query.shape
    depth = min(256, width)
    slots = 8
    count = sum(p.shape[0] for p in hidden_pieces)
    targets = places.shape[0]
    return pl.pallas_call(
        functools.partial(
            project_kernel,
            pieces=len(hidden_pieces),
            heads=heads,
            kv=kv,
            stride=stride,
            depth=depth,
            slots=slots,
        ),
        out_shape=[jax.ShapeDtypeStruct((row_count * stride, LANES), jnp.float32)] * targets,
        in_specs=[smem(), pl.BlockSpec(memory_space=pl.ANY)]
        + [vmem()] * (2 + len(hidden_pieces)),
        out_specs=[vmem()] * targets,
        scratch_shapes=[
            pltpu.VMEM((count, width), jnp.bfloat16),
            pltpu.VMEM((count, columns), jnp.float32),
            pltpu.VMEM((count * stride, LANES), jnp.float32),
            pltpu.VMEM((slots, depth, columns), jnp.bfloat16),
            pltpu.SemaphoreType.DMA((slots,)),
        ],
        compiler_params=pltpu.CompilerParams(vmem_limit_bytes=24 * MIB),
        cost_estimate=pl.CostEstimate(
            flops=1000, bytes_accessed=1000, transcendentals=0
        ),
        name="project",
    )(
        places,
        pltpu.with_memory_space_constraint(w_query, pltpu.HBM),
        pltpu.with_memory_space_constraint(key_weight, pltpu.VMEM),
        pltpu.with_memory_space_constraint(value_weight, pltpu.VMEM),
        *hidden_pieces,
    )


def relay_kernel(*refs):
    half = len(refs) // 2
    for source, target in zip(refs[:half], refs[half:], strict=True):
        target[...] = source[...]


def relay(arrays, microseconds):
    return pl.pallas_call(
        relay_kernel,
        out_shape=[jax.ShapeDtypeStruct(a.shape, a.dtype) for a in arrays],
        in_specs=[vmem()] * len(arrays),
        out_specs=[vmem()] * len(arrays),
        compiler_params=pltpu.CompilerParams(vmem_limit_bytes=8 * MIB),
        cost_estimate=pl.CostEstimate(
            flops=int(microseconds * 1.15e9), bytes_accessed=1 << 16, transcendentals=0
        ),
        name="relay",
    )(*arrays)


def attend_kernel(lengths, cosine, sine, key_cache, cached_values, *refs, heads, kv, stride):
    parts, out = refs[:-1], refs[-1]
    row_count, _, slots, head_dim = key_cache.shape
    per = heads // kv
    scale = head_dim ** (-0.5)
    half = head_dim // 2
    position = lax.broadcasted_iota(jnp.int32, (per, slots), 1)
    for r in range(row_count):
        span = slice(r * stride, (r + 1) * stride)
        summed = parts[0][span, :]
        for p in parts[1:]:
            summed = summed + p[span, :]
        cos_row, sin_row = cosine[r : r + 1, :], sine[r : r + 1, :]
        turned = jnp.concatenate([summed[:, half:], summed[:, :half]], 1)
        rotated = (summed * cos_row + turned * sin_row).astype(jnp.bfloat16)
        inside = position < lengths[r]
        for g in range(kv):
            query = rotated[g * per : (g + 1) * per]
            key_new = rotated[heads + g : heads + g + 1].astype(jnp.float32)
            value_new = summed[heads + kv + g : heads + kv + g + 1].astype(jnp.bfloat16)
            scores = (
                lax.dot_general(
                    query,
                    key_cache[r, g],
                    (((1,), (1,)), ((), ())),
                    preferred_element_type=jnp.float32,
                )
                * scale
            )
            self_score = jnp.sum(query.astype(jnp.float32) * key_new, -1, keepdims=True) * scale
            masked = jnp.where(inside, scores, -jnp.inf)
            highest = jnp.maximum(jnp.max(masked, -1, keepdims=True), self_score)
            weights = jnp.exp(masked - highest)
            self_weight = jnp.exp(self_score - highest)
            denominator = jnp.sum(weights, -1, keepdims=True) + self_weight
            mixed = jnp.dot(
                weights.astype(jnp.bfloat16),
                cached_values[r, g],
                preferred_element_type=jnp.float32,
            )
            mixed = mixed + self_weight.astype(jnp.bfloat16).astype(
                jnp.float32
            ) * value_new.astype(jnp.float32)
            start = r * heads + g * per
            out[start : start + per, :] = (mixed / denominator).astype(jnp.bfloat16)


def attend(lengths, cosine, sine, key_cache, cached_values, parts, heads, kv):
    row_count = key_cache.shape[0]
    stride = parts[0].shape[0] // row_count
    return pl.pallas_call(
        functools.partial(attend_kernel, heads=heads, kv=kv, stride=stride),
        out_shape=jax.ShapeDtypeStruct((row_count * heads, LANES), jnp.bfloat16),
        in_specs=[smem()] + [vmem()] * (4 + len(parts)),
        out_specs=vmem(),
        compiler_params=pltpu.CompilerParams(vmem_limit_bytes=16 * MIB),
        cost_estimate=pl.CostEstimate(flops=1000, bytes_accessed=1000, transcendentals=0),
        name="attend",
    )(
        lengths,
        cosine,
        sine,
        pltpu.with_memory_space_constraint(key_cache, pltpu.VMEM),
        pltpu.with_memory_space_constraint(cached_values, pltpu.VMEM),
        *parts,
    )


def output_kernel(places, w_out, *refs, pieces, heads, rows_out):
    inputs, refs = refs[:pieces], refs[pieces:]
    outs, (laid, rows, total) = refs[:-3], refs[-3:]
    for t, piece in enumerate(inputs):
        laid[places[t]] = piece[...].astype(jnp.float32)
    flat = laid.reshape(laid.shape[0] * laid.shape[1], LANES)
    count = rows.shape[0]
    group = min(8, count)
    for base in range(0, count, group):
        for h in range(heads):
            total[base : base + group, h * LANES : (h + 1) * LANES] = flat[
                pl.ds(base * heads + h, group, stride=heads), :
            ]
    rows[...] = total[...].astype(jnp.bfloat16)
    columns = w_out.shape[1]
    step = min(1024, columns)
    for j in range(0, columns, step):
        sums = jnp.dot(rows[...], w_out[:, j : j + step], preferred_element_type=jnp.float32)
        for s, out in enumerate(outs):
            out[:, j : j + step] = sums[s * rows_out : (s + 1) * rows_out, :]


def output(places, pieces, w_out, row_count, heads, rows_out, targets):
    count = row_count * len(pieces)
    width, columns = w_out.shape
    return pl.pallas_call(
        functools.partial(output_kernel, pieces=len(pieces), heads=heads, rows_out=rows_out),
        out_shape=[jax.ShapeDtypeStruct((rows_out, columns), jnp.float32)] * targets,
        in_specs=[smem()] + [vmem()] * (1 + len(pieces)),
        out_specs=[vmem()] * targets,
        scratch_shapes=[
            pltpu.VMEM((len(pieces), row_count * heads, LANES), jnp.float32),
            pltpu.VMEM((count, width), jnp.bfloat16),
            pltpu.VMEM((count, max(width, columns)), jnp.float32),
        ],
        compiler_params=pltpu.CompilerParams(vmem_limit_bytes=16 * MIB),
        cost_estimate=pl.CostEstimate(flops=1000, bytes_accessed=1000, transcendentals=0),
        name="output",
    )(places, pltpu.with_memory_space_constraint(w_out, pltpu.VMEM), *pieces)


def rotation(lengths, head_dim):
    half = head_dim // 2
    exponents = jnp.arange(half, dtype=jnp.float32) * (2.0 / head_dim)
    frequency = jnp.exp(-math.log(THETA) * exponents)
    angles = lengths.astype(jnp.float32)[:, None] * frequency[None, :]
    cosine, sine = jnp.cos(angles), jnp.sin(angles)
    return jnp.concatenate([cosine, cosine], 1), jnp.concatenate([-sine, sine], 1)


def body(
    hidden,
    lengths,
    w_query,
    key_weight,
    value_weight,
    w_out,
    key_cache,
    cached_values,
    *,
    wide,
    narrow,
):
    row_count, kv, _, head_dim = key_cache.shape
    heads = w_query.shape[1] // head_dim
    rows_out = hidden.shape[0]
    me_wide, me_narrow = lax.axis_index("wide"), lax.axis_index("narrow")
    blocks = rows_out // row_count

    cosine, sine = rotation(lengths, head_dim)
    hidden_pieces = gather_pieces(hidden, "narrow", narrow)

    starts = []
    for t in range(wide):
        first = peer(me_wide, t, wide) * row_count
        place = first // rows_out
        place = me_narrow ^ place if direct(narrow) else place
        starts.append(place * rows_out + first % rows_out)
    starts = jnp.stack(starts).astype(jnp.int32)
    parts = project(
        starts, hidden_pieces, w_query, key_weight, value_weight, row_count, heads, kv
    )
    parts = relay(parts, 100)
    parts = scatter_pieces(parts, "wide", wide)
    context = attend(lengths, cosine, sine, key_cache, cached_values, parts, heads, kv)
    context_pieces = gather_pieces(context, "wide", wide)

    spots = []
    for t in range(wide):
        owner = peer(me_wide, t, wide)
        target = owner // blocks
        target = me_narrow ^ target if direct(narrow) else target
        spots.append(target * blocks + owner % blocks)
    spots = jnp.stack(spots).astype(jnp.int32)
    sums = output(spots, context_pieces, w_out, row_count, heads, rows_out, narrow)
    sums = scatter_pieces(sums, "narrow", narrow)
    result = sums[0]
    for s in sums[1:]:
        result = result + s
    return result.astype(jnp.bfloat16)


def solution(mesh):
    in_specs = (
        P(("groups", "narrow"), "wide"),
        P(("groups", "wide")),
        P("wide", "narrow"),
        P("wide", "narrow"),
        P("wide", "narrow"),
        P("narrow", "wide"),
        P(("groups", "wide"), "narrow", None, None),
        P(("groups", "wide"), "narrow", None, None),
    )
    return jax.shard_map(
        functools.partial(body, wide=mesh.shape["wide"], narrow=mesh.shape["narrow"]),
        mesh=mesh,
        in_specs=in_specs,
        out_specs=P(("groups", "narrow"), "wide"),
        check_vma=False,
    )
```

```python
import functools
import math

import jax
import jax.numpy as jnp
from jax import lax
from jax.experimental import pallas as pl
from jax.experimental.pallas import tpu as pltpu
from jax.sharding import PartitionSpec as P

MIB = 1 << 20
LANES = 128
THETA = 500000.0
DIRECT_PEERS = 8


def xor_pairs(count, step):
    return [(i, i ^ step) for i in range(count)]


def direct(count):
    return count <= DIRECT_PEERS and count & (count - 1) == 0


def gather_pieces(piece, axis, count):
    if direct(count):
        return [piece] + [lax.ppermute(piece, axis, xor_pairs(count, t)) for t in range(1, count)]
    whole = lax.all_gather(piece, axis, axis=0, tiled=False)
    return [whole[t] for t in range(count)]


def scatter_pieces(pieces, axis, count):
    if direct(count):
        return [pieces[0]] + [
            lax.ppermute(pieces[t], axis, xor_pairs(count, t)) for t in range(1, count)
        ]
    return [lax.psum_scatter(jnp.stack(pieces), axis, scatter_dimension=0, tiled=False)]


def peer(me, t, count):
    return lax.bitwise_xor(me, t) if direct(count) else jnp.int32(t)


def vmem():
    return pl.BlockSpec(memory_space=pltpu.VMEM)


def smem():
    return pl.BlockSpec(memory_space=pltpu.SMEM)


def project_kernel(
    w_query, key_weight, value_weight, *refs, pieces, heads, kv, stride, depth, slots, place
):
    inputs, refs = refs[:pieces], refs[pieces:]
    outs, (rows, total, laid, held, fresh_held, sems, fresh_sems) = refs[:-7], refs[-7:]
    width, columns = w_query.shape
    chunks = width // depth

    def copy(i):
        return pltpu.make_async_copy(
            w_query.at[pl.ds(i * depth, depth)], held.at[i % slots], sems.at[i % slots]
        )

    fresh_copies = [
        pltpu.make_async_copy(w, fresh_held.at[i], fresh_sems.at[i])
        for i, w in enumerate((key_weight, value_weight))
    ]
    for c in fresh_copies:
        c.start()
    for i in range(min(slots, chunks)):
        copy(i).start()
    rows[...] = jnp.concatenate([p[...].astype(jnp.float32) for p in inputs], 0).astype(
        jnp.bfloat16
    )
    count = rows.shape[0]
    group = min(8, count)
    fresh = []
    for i, c in enumerate(fresh_copies):
        c.wait()
        fresh.append(jnp.dot(rows[...], fresh_held[i], preferred_element_type=jnp.float32))
    for i in range(chunks):
        copy(i).wait()
        term = jnp.dot(
            rows[:, i * depth : (i + 1) * depth],
            held[i % slots],
            preferred_element_type=jnp.float32,
        )
        total[...] = term if i == 0 else total[...] + term
        if i + slots < chunks:
            copy(i + slots).start()
    for base in range(0, count, group):
        for h in range(heads + 2 * kv):
            if h < heads:
                block = total[base : base + group, h * LANES : (h + 1) * LANES]
            else:
                which, j = divmod(h - heads, kv)
                block = fresh[which][base : base + group, j * LANES : (j + 1) * LANES]
            laid[pl.ds(base * stride + h, group, stride=stride), :] = block
    for t, out in enumerate(outs):
        out[...] = laid[pl.ds(pl.multiple_of(place(t) * stride, 8), out.shape[0]), :]


def project(place, hidden_pieces, w_query, key_weight, value_weight, targets, row_count, heads, kv):
    stride = -(-(heads + 2 * kv) // 8) * 8
    width, columns = w_query.shape
    depth = min(256, width)
    slots = 6
    count = sum(p.shape[0] for p in hidden_pieces)
    return pl.pallas_call(
        functools.partial(
            project_kernel,
            pieces=len(hidden_pieces),
            heads=heads,
            kv=kv,
            stride=stride,
            depth=depth,
            slots=slots,
            place=place,
        ),
        out_shape=[jax.ShapeDtypeStruct((row_count * stride, LANES), jnp.float32)] * targets,
        in_specs=[pl.BlockSpec(memory_space=pltpu.HBM)] * 3 + [vmem()] * len(hidden_pieces),
        out_specs=[vmem()] * targets,
        scratch_shapes=[
            pltpu.VMEM((count, width), jnp.bfloat16),
            pltpu.VMEM((count, columns), jnp.float32),
            pltpu.VMEM((count * stride, LANES), jnp.float32),
            pltpu.VMEM((slots, depth, columns), jnp.bfloat16),
            pltpu.VMEM((2,) + key_weight.shape, jnp.bfloat16),
            pltpu.SemaphoreType.DMA((slots,)),
            pltpu.SemaphoreType.DMA((2,)),
        ],
        compiler_params=pltpu.CompilerParams(vmem_limit_bytes=18 * MIB),
        cost_estimate=pl.CostEstimate(
            flops=1000, bytes_accessed=1000, transcendentals=0
        ),
        name="project",
    )(
        *(pltpu.with_memory_space_constraint(w, pltpu.HBM) for w in (w_query, key_weight, value_weight)),
        *hidden_pieces,
    )


def relay_kernel(*refs):
    half = len(refs) // 2
    for source, target in zip(refs[:half], refs[half:], strict=True):
        target[...] = source[...]


def relay(arrays, microseconds):
    return pl.pallas_call(
        relay_kernel,
        out_shape=[jax.ShapeDtypeStruct(a.shape, a.dtype) for a in arrays],
        in_specs=[vmem()] * len(arrays),
        out_specs=[vmem()] * len(arrays),
        compiler_params=pltpu.CompilerParams(vmem_limit_bytes=2 * MIB),
        cost_estimate=pl.CostEstimate(
            flops=int(microseconds * 1.15e9), bytes_accessed=1 << 16, transcendentals=0
        ),
        name="relay",
    )(*arrays)


def attend_kernel(lengths, cosine, sine, key_cache, cached_values, *refs, heads, kv, stride):
    parts, out = refs[:-1], refs[-1]
    row_count, _, slots, head_dim = key_cache.shape
    per = heads // kv
    scale = head_dim ** (-0.5)
    half = head_dim // 2
    position = lax.broadcasted_iota(jnp.int32, (per, slots), 1)
    for r in range(row_count):
        span = slice(r * stride, (r + 1) * stride)
        summed = parts[0][span, :]
        for p in parts[1:]:
            summed = summed + p[span, :]
        cos_row, sin_row = cosine[r : r + 1, :], sine[r : r + 1, :]
        turned = jnp.concatenate([summed[:, half:], summed[:, :half]], 1)
        rotated = (summed * cos_row + turned * sin_row).astype(jnp.bfloat16)
        inside = position < lengths[r]
        for g in range(kv):
            query = rotated[g * per : (g + 1) * per]
            key_new = rotated[heads + g : heads + g + 1].astype(jnp.float32)
            value_new = summed[heads + kv + g : heads + kv + g + 1].astype(jnp.bfloat16)
            scores = (
                lax.dot_general(
                    query,
                    key_cache[r, g],
                    (((1,), (1,)), ((), ())),
                    preferred_element_type=jnp.float32,
                )
                * scale
            )
            self_score = jnp.sum(query.astype(jnp.float32) * key_new, -1, keepdims=True) * scale
            masked = jnp.where(inside, scores, -jnp.inf)
            highest = jnp.maximum(jnp.max(masked, -1, keepdims=True), self_score)
            weights = jnp.exp(masked - highest)
            self_weight = jnp.exp(self_score - highest)
            denominator = jnp.sum(weights, -1, keepdims=True) + self_weight
            mixed = jnp.dot(
                weights.astype(jnp.bfloat16),
                cached_values[r, g],
                preferred_element_type=jnp.float32,
            )
            mixed = mixed + self_weight.astype(jnp.bfloat16).astype(
                jnp.float32
            ) * value_new.astype(jnp.float32)
            start = r * heads + g * per
            out[start : start + per, :] = (mixed / denominator).astype(jnp.bfloat16)


def attend(lengths, cosine, sine, key_cache, cached_values, parts, heads, kv):
    row_count = key_cache.shape[0]
    stride = parts[0].shape[0] // row_count
    return pl.pallas_call(
        functools.partial(attend_kernel, heads=heads, kv=kv, stride=stride),
        out_shape=jax.ShapeDtypeStruct((row_count * heads, LANES), jnp.bfloat16),
        in_specs=[smem()] + [vmem()] * (4 + len(parts)),
        out_specs=vmem(),
        compiler_params=pltpu.CompilerParams(vmem_limit_bytes=6 * MIB),
        cost_estimate=pl.CostEstimate(flops=1000, bytes_accessed=1000, transcendentals=0),
        name="attend",
    )(
        lengths,
        cosine,
        sine,
        key_cache,
        cached_values,
        *parts,
    )


def arrange_kernel(*refs, pieces, heads, place):
    inputs, (rows, laid, total) = refs[:pieces], refs[pieces:]
    for t, piece in enumerate(inputs):
        laid[place(t)] = piece[...].astype(jnp.float32)
    flat = laid.reshape(laid.shape[0] * laid.shape[1], LANES)
    count = rows.shape[0]
    group = min(8, count)
    for base in range(0, count, group):
        for h in range(heads):
            total[base : base + group, h * LANES : (h + 1) * LANES] = flat[
                pl.ds(base * heads + h, group, stride=heads), :
            ]
    rows[...] = total[...].astype(jnp.bfloat16)


def arrange(place, pieces, row_count, heads):
    count = row_count * len(pieces)
    return pl.pallas_call(
        functools.partial(arrange_kernel, pieces=len(pieces), heads=heads, place=place),
        out_shape=jax.ShapeDtypeStruct((count, heads * LANES), jnp.bfloat16),
        in_specs=[vmem()] * len(pieces),
        out_specs=vmem(),
        scratch_shapes=[
            pltpu.VMEM((len(pieces), row_count * heads, LANES), jnp.float32),
            pltpu.VMEM((count, heads * LANES), jnp.float32),
        ],
        compiler_params=pltpu.CompilerParams(vmem_limit_bytes=6 * MIB),
        cost_estimate=pl.CostEstimate(flops=1000, bytes_accessed=1000, transcendentals=0),
        name="arrange",
    )(*pieces)


def output_kernel(rows, w_out, *outs, rows_out):
    columns = w_out.shape[1]
    step = min(1024, columns)
    for j in range(0, columns, step):
        sums = jnp.dot(rows[...], w_out[:, j : j + step], preferred_element_type=jnp.float32)
        for s, out in enumerate(outs):
            out[:, j : j + step] = sums[s * rows_out : (s + 1) * rows_out, :]


def output(rows, w_out, rows_out, targets):
    columns = w_out.shape[1]
    return pl.pallas_call(
        functools.partial(output_kernel, rows_out=rows_out),
        out_shape=[jax.ShapeDtypeStruct((rows_out, columns), jnp.float32)] * targets,
        in_specs=[vmem()] * 2,
        out_specs=[vmem()] * targets,
        compiler_params=pltpu.CompilerParams(vmem_limit_bytes=20 * MIB),
        cost_estimate=pl.CostEstimate(flops=1000, bytes_accessed=1000, transcendentals=0),
        name="output",
    )(rows, w_out)


def rotation(lengths, head_dim):
    half = head_dim // 2
    exponents = jnp.arange(half, dtype=jnp.float32) * (2.0 / head_dim)
    frequency = jnp.exp(-math.log(THETA) * exponents)
    angles = lengths.astype(jnp.float32)[:, None] * frequency[None, :]
    cosine, sine = jnp.cos(angles), jnp.sin(angles)
    return jnp.concatenate([cosine, cosine], 1), jnp.concatenate([-sine, sine], 1)


def body(
    hidden,
    lengths,
    w_query,
    key_weight,
    value_weight,
    w_out,
    key_cache,
    cached_values,
    *,
    wide,
    narrow,
):
    row_count, kv, _, head_dim = key_cache.shape
    heads = w_query.shape[1] // head_dim
    rows_out = hidden.shape[0]
    blocks = rows_out // row_count

    def target(owner):
        first, rest = lax.div(owner, blocks), lax.rem(owner, blocks)
        if direct(narrow):
            first = lax.bitwise_xor(lax.axis_index("narrow"), first)
        return first * blocks + rest

    def place(t):
        return target(peer(lax.axis_index("wide"), t, wide))

    cosine, sine = rotation(lengths, head_dim)
    hidden_pieces = gather_pieces(hidden, "narrow", narrow)
    parts = project(
        lambda t: place(t) * row_count,
        hidden_pieces,
        w_query,
        key_weight,
        value_weight,
        wide,
        row_count,
        heads,
        kv,
    )
    *parts, cosine, sine = relay([*parts, cosine, sine], 100)
    parts = scatter_pieces(parts, "wide", wide)
    context = attend(lengths, cosine, sine, key_cache, cached_values, parts, heads, kv)
    context_pieces = gather_pieces(context, "wide", wide)
    rows = arrange(place, context_pieces, row_count, heads)
    sums = output(rows, w_out, rows_out, narrow)
    sums = scatter_pieces(sums, "narrow", narrow)
    result = sums[0]
    for s in sums[1:]:
        result = result + s
    return result.astype(jnp.bfloat16)


def solution(mesh):
    in_specs = (
        P(("groups", "narrow"), "wide"),
        P(("groups", "wide")),
        P("wide", "narrow"),
        P("wide", "narrow"),
        P("wide", "narrow"),
        P("narrow", "wide"),
        P(("groups", "wide"), "narrow", None, None),
        P(("groups", "wide"), "narrow", None, None),
    )
    return jax.shard_map(
        functools.partial(body, wide=mesh.shape["wide"], narrow=mesh.shape["narrow"]),
        mesh=mesh,
        in_specs=in_specs,
        out_specs=P(("groups", "narrow"), "wide"),
        check_vma=False,
    )
```

```python
import functools
import math

import jax
import jax.numpy as jnp
from jax import lax
from jax.experimental import pallas as pl
from jax.experimental.pallas import tpu as pltpu
from jax.sharding import PartitionSpec as P

MIB = 1 << 20
LANES = 128
THETA = 500000.0
HEAD_SHARE = 4
LOADS = 4
SLOTS = 6
CUTS = 2
DIRECT_PEERS = 8


def xor_pairs(count, step):
    return [(i, i ^ step) for i in range(count)]


def direct(count):
    return count <= DIRECT_PEERS and count & (count - 1) == 0


def gather_pieces(piece, axis, count):
    if direct(count):
        return [piece] + [lax.ppermute(piece, axis, xor_pairs(count, t)) for t in range(1, count)]
    whole = lax.all_gather(piece, axis, axis=0, tiled=False)
    return [whole[t] for t in range(count)]


def scatter_pieces(pieces, axis, count):
    if direct(count):
        arrived = [
            lax.ppermute(pieces[t], axis, xor_pairs(count, t)) for t in reversed(range(1, count))
        ]
        return [pieces[0]] + arrived
    return [lax.psum_scatter(jnp.stack(pieces), axis, scatter_dimension=0, tiled=False)]


def peer(me, t, count):
    return lax.bitwise_xor(me, t) if direct(count) else jnp.int32(t)


def vmem():
    return pl.BlockSpec(memory_space=pltpu.VMEM)


def smem():
    return pl.BlockSpec(memory_space=pltpu.SMEM)


def collect_kernel(*refs):
    refs[-1][...] = jnp.concatenate([r[...].astype(jnp.float32) for r in refs[:-1]], 0).astype(
        jnp.bfloat16
    )


def collect(pieces):
    count = sum(p.shape[0] for p in pieces)
    return pl.pallas_call(
        collect_kernel,
        out_shape=jax.ShapeDtypeStruct((count, pieces[0].shape[1]), jnp.bfloat16),
        in_specs=[vmem()] * len(pieces),
        out_specs=vmem(),
        compiler_params=pltpu.CompilerParams(vmem_limit_bytes=6 * MIB),
        cost_estimate=pl.CostEstimate(flops=1000, bytes_accessed=1000, transcendentals=0),
        name="collect",
    )(*pieces)


def head_depth(w_query):
    return w_query.shape[0] // HEAD_SHARE


def load_kernel(w_query, key_weight, value_weight, head, sems):
    del key_weight, value_weight
    depth = head.shape[0] // LOADS
    copies = [
        pltpu.make_async_copy(
            w_query.at[pl.ds(i * depth, depth)], head.at[pl.ds(i * depth, depth)], sems.at[i]
        )
        for i in range(LOADS)
    ]
    for copy in copies:
        copy.start()
    for copy in copies:
        copy.wait()


def load(w_query, key_weight, value_weight):
    shape = (head_depth(w_query), w_query.shape[1])
    return pl.pallas_call(
        load_kernel,
        out_shape=jax.ShapeDtypeStruct(shape, w_query.dtype),
        in_specs=[pl.BlockSpec(memory_space=pltpu.HBM), vmem(), vmem()],
        out_specs=vmem(),
        scratch_shapes=[pltpu.SemaphoreType.DMA((LOADS,))],
        compiler_params=pltpu.CompilerParams(vmem_limit_bytes=2 * MIB),
        cost_estimate=pl.CostEstimate(
            flops=1000, bytes_accessed=2 * math.prod(shape), transcendentals=0
        ),
        name="load",
    )(pltpu.with_memory_space_constraint(w_query, pltpu.HBM), key_weight, value_weight)


def project_kernel(
    rows, head, key_weight, value_weight, w_query, *refs, heads, kv, stride, place, depth, slots
):
    outs, (total, laid, held, sems) = refs[:-4], refs[-4:]
    count, width = rows.shape
    done = head.shape[0]
    cut = held.shape[2]
    cuts = w_query.shape[1] // cut
    chunks = (width - done) // depth * cuts
    group = min(8, count)

    def copy(i):
        start, first = done + i // cuts * depth, i % cuts * cut
        return pltpu.make_async_copy(
            w_query.at[pl.ds(start, depth), pl.ds(first, cut)],
            held.at[i % slots],
            sems.at[i % slots],
        )

    def lay(sums, first):
        for base in range(0, count, group):
            for h in range(sums.shape[1] // LANES):
                laid[pl.ds(base * stride + first + h, group, stride=stride), :] = sums[
                    base : base + group, h * LANES : (h + 1) * LANES
                ]

    for i in range(min(slots, chunks)):
        copy(i).start()
    half = width // 2
    for i, w in enumerate((key_weight, value_weight)):
        lay(
            jnp.dot(rows[:, :half], w[:half], preferred_element_type=jnp.float32)
            + jnp.dot(rows[:, half:], w[half:], preferred_element_type=jnp.float32),
            heads + i * kv,
        )
    total[...] = jnp.dot(rows[:, :done], head[...], preferred_element_type=jnp.float32)
    for i in range(chunks):
        copy(i).wait()
        start, first = done + i // cuts * depth, i % cuts * cut
        total[:, first : first + cut] += jnp.dot(
            rows[:, start : start + depth], held[i % slots], preferred_element_type=jnp.float32
        )
        if i + slots < chunks:
            copy(i + slots).start()
    lay(total, 0)
    for t, out in enumerate(outs):
        out[...] = laid[pl.ds(pl.multiple_of(place(t) * stride, 8), out.shape[0]), :]


def project(place, rows, head, key_weight, value_weight, w_query, targets, row_count, heads, kv):
    stride = -(-(heads + 2 * kv) // 8) * 8
    count, width = rows.shape
    columns = w_query.shape[1]
    depth = math.gcd(256, width - head.shape[0])
    scratch = SLOTS * depth * (columns // CUTS) * 2 + count * (columns + stride * LANES) * 4
    return pl.pallas_call(
        functools.partial(
            project_kernel,
            heads=heads,
            kv=kv,
            stride=stride,
            place=place,
            depth=depth,
            slots=SLOTS,
        ),
        out_shape=[jax.ShapeDtypeStruct((row_count * stride, LANES), jnp.float32)] * targets,
        in_specs=[vmem()] * 4 + [pl.BlockSpec(memory_space=pltpu.HBM)],
        out_specs=[vmem()] * targets,
        scratch_shapes=[
            pltpu.VMEM((count, columns), jnp.float32),
            pltpu.VMEM((count * stride, LANES), jnp.float32),
            pltpu.VMEM((SLOTS, depth, columns // CUTS), jnp.bfloat16),
            pltpu.SemaphoreType.DMA((SLOTS,)),
        ],
        compiler_params=pltpu.CompilerParams(vmem_limit_bytes=(scratch // MIB + 1 + count // 16) * MIB),
        cost_estimate=pl.CostEstimate(flops=1000, bytes_accessed=1000, transcendentals=0),
        name="project",
    )(
        rows,
        head,
        key_weight,
        value_weight,
        pltpu.with_memory_space_constraint(w_query, pltpu.HBM),
    )


def relay_kernel(*refs):
    half = len(refs) // 2
    for source, target in zip(refs[:half], refs[half:], strict=True):
        target[...] = source[...]


def relay(arrays, microseconds):
    return pl.pallas_call(
        relay_kernel,
        out_shape=[jax.ShapeDtypeStruct(a.shape, a.dtype) for a in arrays],
        in_specs=[vmem()] * len(arrays),
        out_specs=[vmem()] * len(arrays),
        compiler_params=pltpu.CompilerParams(vmem_limit_bytes=2 * MIB),
        cost_estimate=pl.CostEstimate(
            flops=int(microseconds * 1.15e9), bytes_accessed=1 << 16, transcendentals=0
        ),
        name="relay",
    )(*arrays)


def attend_kernel(lengths, cosine, sine, key_cache, cached_values, *refs, heads, kv, stride):
    parts, out = refs[:-1], refs[-1]
    row_count, _, slots, head_dim = key_cache.shape
    per = heads // kv
    scale = head_dim ** (-0.5)
    half = head_dim // 2
    position = lax.broadcasted_iota(jnp.int32, (per, slots), 1)
    pairs = [(r, g) for r in range(row_count) for g in range(kv)]
    queries, self_scores, values_new, scores = {}, {}, {}, {}
    for r in range(row_count):
        span = slice(r * stride, (r + 1) * stride)
        summed = parts[0][span, :]
        for p in parts[1:]:
            summed = summed + p[span, :]
        cos_row, sin_row = cosine[r : r + 1, :], sine[r : r + 1, :]
        turned = jnp.concatenate([summed[:, half:], summed[:, :half]], 1)
        rotated = (summed * cos_row + turned * sin_row).astype(jnp.bfloat16)
        for g in range(kv):
            queries[r, g] = rotated[g * per : (g + 1) * per]
            key_new = rotated[heads + g : heads + g + 1].astype(jnp.float32)
            self_scores[r, g] = (
                jnp.sum(queries[r, g].astype(jnp.float32) * key_new, -1, keepdims=True) * scale
            )
            values_new[r, g] = summed[heads + kv + g : heads + kv + g + 1].astype(jnp.bfloat16)
    for r, g in pairs:
        scores[r, g] = lax.dot_general(
            queries[r, g],
            key_cache[r, g],
            (((1,), (1,)), ((), ())),
            preferred_element_type=jnp.float32,
        )
    weights, self_weights, denominators = {}, {}, {}
    for r, g in pairs:
        masked = jnp.where(position < lengths[r], scores[r, g] * scale, -jnp.inf)
        highest = jnp.maximum(jnp.max(masked, -1, keepdims=True), self_scores[r, g])
        raised = jnp.exp(masked - highest)
        self_weight = jnp.exp(self_scores[r, g] - highest)
        denominators[r, g] = jnp.sum(raised, -1, keepdims=True) + self_weight
        weights[r, g] = raised.astype(jnp.bfloat16)
        self_weights[r, g] = self_weight.astype(jnp.bfloat16).astype(jnp.float32)
    for r, g in pairs:
        mixed = jnp.dot(
            weights[r, g], cached_values[r, g], preferred_element_type=jnp.float32
        ) + self_weights[r, g] * values_new[r, g].astype(jnp.float32)
        start = r * heads + g * per
        out[start : start + per, :] = (mixed / denominators[r, g]).astype(jnp.bfloat16)


def attend(lengths, cosine, sine, key_cache, cached_values, parts, heads, kv):
    row_count = key_cache.shape[0]
    stride = parts[0].shape[0] // row_count
    return pl.pallas_call(
        functools.partial(attend_kernel, heads=heads, kv=kv, stride=stride),
        out_shape=jax.ShapeDtypeStruct((row_count * heads, LANES), jnp.bfloat16),
        in_specs=[smem()] + [vmem()] * (4 + len(parts)),
        out_specs=vmem(),
        compiler_params=pltpu.CompilerParams(vmem_limit_bytes=6 * MIB),
        cost_estimate=pl.CostEstimate(flops=1000, bytes_accessed=1000, transcendentals=0),
        name="attend",
    )(
        lengths,
        cosine,
        sine,
        key_cache,
        cached_values,
        *parts,
    )


def arrange_kernel(*refs, pieces, heads, place):
    inputs, (rows, laid, total) = refs[:pieces], refs[pieces:]
    for t, piece in enumerate(inputs):
        laid[place(t)] = piece[...].astype(jnp.float32)
    flat = laid.reshape(laid.shape[0] * laid.shape[1], LANES)
    count = rows.shape[0]
    group = min(8, count)
    for base in range(0, count, group):
        for h in range(heads):
            total[base : base + group, h * LANES : (h + 1) * LANES] = flat[
                pl.ds(base * heads + h, group, stride=heads), :
            ]
    rows[...] = total[...].astype(jnp.bfloat16)


def arrange(place, pieces, row_count, heads):
    count = row_count * len(pieces)
    return pl.pallas_call(
        functools.partial(arrange_kernel, pieces=len(pieces), heads=heads, place=place),
        out_shape=jax.ShapeDtypeStruct((count, heads * LANES), jnp.bfloat16),
        in_specs=[vmem()] * len(pieces),
        out_specs=vmem(),
        scratch_shapes=[
            pltpu.VMEM((len(pieces), row_count * heads, LANES), jnp.float32),
            pltpu.VMEM((count, heads * LANES), jnp.float32),
        ],
        compiler_params=pltpu.CompilerParams(vmem_limit_bytes=6 * MIB),
        cost_estimate=pl.CostEstimate(flops=1000, bytes_accessed=1000, transcendentals=0),
        name="arrange",
    )(*pieces)


def output_kernel(rows, w_out, *outs, rows_out):
    columns = w_out.shape[1]
    step = min(1024, columns)
    for j in range(0, columns, step):
        sums = jnp.dot(rows[...], w_out[:, j : j + step], preferred_element_type=jnp.float32)
        for s, out in enumerate(outs):
            out[:, j : j + step] = sums[s * rows_out : (s + 1) * rows_out, :]


def output(rows, w_out, rows_out, targets):
    columns = w_out.shape[1]
    return pl.pallas_call(
        functools.partial(output_kernel, rows_out=rows_out),
        out_shape=[jax.ShapeDtypeStruct((rows_out, columns), jnp.float32)] * targets,
        in_specs=[vmem()] * 2,
        out_specs=[vmem()] * targets,
        compiler_params=pltpu.CompilerParams(vmem_limit_bytes=20 * MIB),
        cost_estimate=pl.CostEstimate(flops=1000, bytes_accessed=1000, transcendentals=0),
        name="output",
    )(rows, w_out)


def frequency_kernel(out):
    head_dim = out.shape[1]
    lane = lax.broadcasted_iota(jnp.int32, out.shape, 1)
    exponents = (lane % (head_dim // 2)).astype(jnp.float32) * (2.0 / head_dim)
    out[...] = jnp.exp(-math.log(THETA) * exponents)


def frequencies(head_dim, microseconds):
    return pl.pallas_call(
        frequency_kernel,
        out_shape=jax.ShapeDtypeStruct((8, head_dim), jnp.float32),
        out_specs=vmem(),
        compiler_params=pltpu.CompilerParams(vmem_limit_bytes=2 * MIB),
        cost_estimate=pl.CostEstimate(
            flops=int(microseconds * 1.15e9), bytes_accessed=1 << 16, transcendentals=0
        ),
        name="frequencies",
    )()


def rotation(lengths, frequency):
    angles = lengths.astype(jnp.float32)[:, None] * frequency[:1]
    half = frequency.shape[1] // 2
    sine = jnp.sin(angles)
    return jnp.cos(angles), jnp.where(jnp.arange(2 * half) < half, -sine, sine)


def body(
    hidden,
    lengths,
    w_query,
    key_weight,
    value_weight,
    w_out,
    key_cache,
    cached_values,
    *,
    wide,
    narrow,
):
    row_count, kv, _, head_dim = key_cache.shape
    heads = w_query.shape[1] // head_dim
    rows_out = hidden.shape[0]
    blocks = rows_out // row_count

    def target(owner):
        first, rest = lax.div(owner, blocks), lax.rem(owner, blocks)
        if direct(narrow):
            first = lax.bitwise_xor(lax.axis_index("narrow"), first)
        return first * blocks + rest

    def place(t):
        return target(peer(lax.axis_index("wide"), t, wide))

    frequency, hidden = lax.optimization_barrier((frequencies(head_dim, 100), hidden))
    cosine, sine = rotation(lengths, frequency)
    hidden_pieces = gather_pieces(hidden, "narrow", narrow)
    parts = project(
        lambda t: place(t) * row_count,
        collect(hidden_pieces),
        load(w_query, key_weight, value_weight),
        key_weight,
        value_weight,
        w_query,
        wide,
        row_count,
        heads,
        kv,
    )
    *parts, cosine, sine = relay(relay([*parts, cosine, sine], 0), 100)
    parts = scatter_pieces(parts, "wide", wide)
    context = attend(lengths, cosine, sine, key_cache, cached_values, parts, heads, kv)
    context_pieces = gather_pieces(context, "wide", wide)
    rows = arrange(place, context_pieces, row_count, heads)
    sums = output(rows, w_out, rows_out, narrow)
    sums = scatter_pieces(sums, "narrow", narrow)
    result = sums[0]
    for s in sums[1:]:
        result = result + s
    return result.astype(jnp.bfloat16)


def solution(mesh):
    in_specs = (
        P(("groups", "narrow"), "wide"),
        P(("groups", "wide")),
        P("wide", "narrow"),
        P("wide", "narrow"),
        P("wide", "narrow"),
        P("narrow", "wide"),
        P(("groups", "wide"), "narrow", None, None),
        P(("groups", "wide"), "narrow", None, None),
    )
    return jax.shard_map(
        functools.partial(body, wide=mesh.shape["wide"], narrow=mesh.shape["narrow"]),
        mesh=mesh,
        in_specs=in_specs,
        out_specs=P(("groups", "narrow"), "wide"),
        check_vma=False,
    )
```

```python
import functools
import math

import jax
import jax.numpy as jnp
from jax import lax
from jax.experimental import pallas as pl
from jax.experimental.pallas import tpu as pltpu
from jax.sharding import PartitionSpec as P

MIB = 1 << 20
LANES = 128
THETA = 500000.0
HEAD_SHARE = 4
LOADS = 4
SLOTS = 6
CUTS = 2
DIRECT_PEERS = 8


def xor_pairs(count, step):
    return [(i, i ^ step) for i in range(count)]


def direct(count):
    return count <= DIRECT_PEERS and count & (count - 1) == 0


def gather_pieces(piece, axis, count):
    if direct(count):
        return [piece] + [lax.ppermute(piece, axis, xor_pairs(count, t)) for t in range(1, count)]
    whole = lax.all_gather(piece, axis, axis=0, tiled=False)
    return [whole[t] for t in range(count)]


def scatter_pieces(pieces, axis, count):
    if direct(count):
        arrived = [
            lax.ppermute(pieces[t], axis, xor_pairs(count, t)) for t in reversed(range(1, count))
        ]
        return [pieces[0]] + arrived
    return [lax.psum_scatter(jnp.stack(pieces), axis, scatter_dimension=0, tiled=False)]


def peer(me, t, count):
    return lax.bitwise_xor(me, t) if direct(count) else jnp.int32(t)


def smem():
    return pl.BlockSpec(memory_space=pltpu.SMEM)


def vmem():
    return pl.BlockSpec(memory_space=pltpu.VMEM)


def head_depth(w_query):
    return w_query.shape[0] // HEAD_SHARE


def load_kernel(w_query, key_weight, value_weight, head, sems):
    del key_weight, value_weight
    depth = head.shape[0] // LOADS
    copies = [
        pltpu.make_async_copy(
            w_query.at[pl.ds(i * depth, depth)], head.at[pl.ds(i * depth, depth)], sems.at[i]
        )
        for i in range(LOADS)
    ]
    for copy in copies:
        copy.start()
    for copy in copies:
        copy.wait()


def load(w_query, key_weight, value_weight):
    shape = (head_depth(w_query), w_query.shape[1])
    return pl.pallas_call(
        load_kernel,
        out_shape=jax.ShapeDtypeStruct(shape, w_query.dtype),
        in_specs=[pl.BlockSpec(memory_space=pltpu.HBM), vmem(), vmem()],
        out_specs=vmem(),
        scratch_shapes=[pltpu.SemaphoreType.DMA((LOADS,))],
        compiler_params=pltpu.CompilerParams(vmem_limit_bytes=2 * MIB),
        cost_estimate=pl.CostEstimate(
            flops=1000, bytes_accessed=2 * math.prod(shape), transcendentals=0
        ),
        name="load",
    )(pltpu.with_memory_space_constraint(w_query, pltpu.HBM), key_weight, value_weight)


def project_kernel(
    head, key_weight, value_weight, w_query, *refs, pieces, heads, kv, stride, place, depth, slots
):
    inputs, refs = refs[:pieces], refs[pieces:]
    outs, (rows, total, laid, held, sems) = refs[:-5], refs[-5:]
    count, width = rows.shape
    done = head.shape[0]
    cut = held.shape[2]
    cuts = w_query.shape[1] // cut
    chunks = (width - done) // depth * cuts
    group = min(8, count)

    def copy(i):
        start, first = done + i // cuts * depth, i % cuts * cut
        return pltpu.make_async_copy(
            w_query.at[pl.ds(start, depth), pl.ds(first, cut)],
            held.at[i % slots],
            sems.at[i % slots],
        )

    def lay(sums, first):
        for base in range(0, count, group):
            for h in range(sums.shape[1] // LANES):
                laid[pl.ds(base * stride + first + h, group, stride=stride), :] = sums[
                    base : base + group, h * LANES : (h + 1) * LANES
                ]

    for i in range(min(slots, chunks)):
        copy(i).start()
    rows[...] = jnp.concatenate([p[...].astype(jnp.float32) for p in inputs], 0).astype(
        jnp.bfloat16
    )
    half = width // 2
    for i, w in enumerate((key_weight, value_weight)):
        lay(
            jnp.dot(rows[:, :half], w[:half], preferred_element_type=jnp.float32)
            + jnp.dot(rows[:, half:], w[half:], preferred_element_type=jnp.float32),
            heads + i * kv,
        )
    total[...] = jnp.dot(rows[:, :done], head[...], preferred_element_type=jnp.float32)
    for i in range(chunks):
        copy(i).wait()
        start, first = done + i // cuts * depth, i % cuts * cut
        total[:, first : first + cut] += jnp.dot(
            rows[:, start : start + depth], held[i % slots], preferred_element_type=jnp.float32
        )
        if i + slots < chunks:
            copy(i + slots).start()
        if i + cuts >= chunks:
            lay(total[:, first : first + cut], first // LANES)
    for t, out in enumerate(outs):
        out[...] = laid[pl.ds(pl.multiple_of(place(t) * stride, 8), out.shape[0]), :]


def project(
    place, hidden_pieces, head, key_weight, value_weight, w_query, targets, row_count, heads, kv
):
    stride = -(-(heads + 2 * kv) // 8) * 8
    width, columns = w_query.shape
    count = sum(p.shape[0] for p in hidden_pieces)
    depth = math.gcd(256, width - head.shape[0])
    scratch = SLOTS * depth * (columns // CUTS) * 2 + count * (columns + stride * LANES) * 4
    return pl.pallas_call(
        functools.partial(
            project_kernel,
            pieces=len(hidden_pieces),
            heads=heads,
            kv=kv,
            stride=stride,
            place=place,
            depth=depth,
            slots=SLOTS,
        ),
        out_shape=[jax.ShapeDtypeStruct((row_count * stride, LANES), jnp.float32)] * targets,
        in_specs=[vmem()] * 3
        + [pl.BlockSpec(memory_space=pltpu.HBM)]
        + [vmem()] * len(hidden_pieces),
        out_specs=[vmem()] * targets,
        scratch_shapes=[
            pltpu.VMEM((count, width), jnp.bfloat16),
            pltpu.VMEM((count, columns), jnp.float32),
            pltpu.VMEM((count * stride, LANES), jnp.float32),
            pltpu.VMEM((SLOTS, depth, columns // CUTS), jnp.bfloat16),
            pltpu.SemaphoreType.DMA((SLOTS,)),
        ],
        compiler_params=pltpu.CompilerParams(vmem_limit_bytes=(scratch // MIB + 1 + count // 16) * MIB),
        cost_estimate=pl.CostEstimate(flops=1000, bytes_accessed=1000, transcendentals=0),
        name="project",
    )(
        head,
        key_weight,
        value_weight,
        pltpu.with_memory_space_constraint(w_query, pltpu.HBM),
        *hidden_pieces,
    )


def relay_kernel(*refs):
    half = len(refs) // 2
    for source, target in zip(refs[:half], refs[half:], strict=True):
        target[...] = source[...]


def relay(arrays, microseconds):
    return pl.pallas_call(
        relay_kernel,
        out_shape=[jax.ShapeDtypeStruct(a.shape, a.dtype) for a in arrays],
        in_specs=[vmem()] * len(arrays),
        out_specs=[vmem()] * len(arrays),
        compiler_params=pltpu.CompilerParams(vmem_limit_bytes=2 * MIB),
        cost_estimate=pl.CostEstimate(
            flops=int(microseconds * 1.15e9), bytes_accessed=1 << 16, transcendentals=0
        ),
        name="relay",
    )(*arrays)


def attend_kernel(limits, cosine, sine, key_cache, cached_values, *refs, heads, kv, stride):
    parts, out = refs[:-1], refs[-1]
    row_count, _, slots, head_dim = key_cache.shape
    per = heads // kv
    scale = head_dim ** (-0.5)
    half = head_dim // 2
    position = lax.broadcasted_iota(jnp.int32, (per, slots), 1)
    pairs = [(r, g) for r in range(row_count) for g in range(kv)]
    queries, self_scores, values_new, scores = {}, {}, {}, {}
    for r in range(row_count):
        span = slice(r * stride, (r + 1) * stride)
        summed = parts[0][span, :]
        for p in parts[1:]:
            summed = summed + p[span, :]
        cos_row, sin_row = cosine[r : r + 1, :], sine[r : r + 1, :]
        turned = jnp.concatenate([summed[:, half:], summed[:, :half]], 1)
        rotated = (summed * cos_row + turned * sin_row).astype(jnp.bfloat16)
        for g in range(kv):
            queries[r, g] = rotated[g * per : (g + 1) * per]
            key_new = rotated[heads + g : heads + g + 1].astype(jnp.float32)
            self_scores[r, g] = (
                jnp.sum(queries[r, g].astype(jnp.float32) * key_new, -1, keepdims=True) * scale
            )
            values_new[r, g] = summed[heads + kv + g : heads + kv + g + 1].astype(jnp.bfloat16)
    for r, g in pairs:
        scores[r, g] = lax.dot_general(
            queries[r, g],
            key_cache[r, g],
            (((1,), (1,)), ((), ())),
            preferred_element_type=jnp.float32,
        )
    weights, self_weights, denominators = {}, {}, {}
    for r, g in pairs:
        masked = jnp.where(position < limits[r : r + 1, :1], scores[r, g] * scale, -jnp.inf)
        highest = jnp.maximum(jnp.max(masked, -1, keepdims=True), self_scores[r, g])
        raised = jnp.exp(masked - highest)
        self_weight = jnp.exp(self_scores[r, g] - highest)
        denominators[r, g] = jnp.sum(raised, -1, keepdims=True) + self_weight
        weights[r, g] = raised.astype(jnp.bfloat16)
        self_weights[r, g] = self_weight.astype(jnp.bfloat16).astype(jnp.float32)
    for r, g in pairs:
        mixed = jnp.dot(
            weights[r, g], cached_values[r, g], preferred_element_type=jnp.float32
        ) + self_weights[r, g] * values_new[r, g].astype(jnp.float32)
        start = r * heads + g * per
        out[start : start + per, :] = (mixed / denominators[r, g]).astype(jnp.bfloat16)


def attend(tables, key_cache, cached_values, parts, heads, kv):
    row_count = key_cache.shape[0]
    stride = parts[0].shape[0] // row_count
    return pl.pallas_call(
        functools.partial(attend_kernel, heads=heads, kv=kv, stride=stride),
        out_shape=jax.ShapeDtypeStruct((row_count * heads, LANES), jnp.bfloat16),
        in_specs=[vmem()] * (5 + len(parts)),
        out_specs=vmem(),
        compiler_params=pltpu.CompilerParams(vmem_limit_bytes=6 * MIB),
        cost_estimate=pl.CostEstimate(flops=1000, bytes_accessed=1000, transcendentals=0),
        name="attend",
    )(
        *tables,
        key_cache,
        cached_values,
        *parts,
    )


def arrange_kernel(*refs, pieces, heads, place):
    inputs, (rows, laid, total) = refs[:pieces], refs[pieces:]
    for t, piece in enumerate(inputs):
        laid[place(t)] = piece[...].astype(jnp.float32)
    flat = laid.reshape(laid.shape[0] * laid.shape[1], LANES)
    count = rows.shape[0]
    group = min(8, count)
    for base in range(0, count, group):
        for h in range(heads):
            total[base : base + group, h * LANES : (h + 1) * LANES] = flat[
                pl.ds(base * heads + h, group, stride=heads), :
            ]
    rows[...] = total[...].astype(jnp.bfloat16)


def arrange(place, pieces, row_count, heads):
    count = row_count * len(pieces)
    return pl.pallas_call(
        functools.partial(arrange_kernel, pieces=len(pieces), heads=heads, place=place),
        out_shape=jax.ShapeDtypeStruct((count, heads * LANES), jnp.bfloat16),
        in_specs=[vmem()] * len(pieces),
        out_specs=vmem(),
        scratch_shapes=[
            pltpu.VMEM((len(pieces), row_count * heads, LANES), jnp.float32),
            pltpu.VMEM((count, heads * LANES), jnp.float32),
        ],
        compiler_params=pltpu.CompilerParams(vmem_limit_bytes=6 * MIB),
        cost_estimate=pl.CostEstimate(flops=1000, bytes_accessed=1000, transcendentals=0),
        name="arrange",
    )(*pieces)


def output_kernel(rows, w_out, *outs, rows_out):
    columns = w_out.shape[1]
    step = min(1024, columns)
    for j in range(0, columns, step):
        sums = jnp.dot(rows[...], w_out[:, j : j + step], preferred_element_type=jnp.float32)
        for s, out in enumerate(outs):
            out[:, j : j + step] = sums[s * rows_out : (s + 1) * rows_out, :]


def output(rows, w_out, rows_out, targets):
    columns = w_out.shape[1]
    return pl.pallas_call(
        functools.partial(output_kernel, rows_out=rows_out),
        out_shape=[jax.ShapeDtypeStruct((rows_out, columns), jnp.float32)] * targets,
        in_specs=[vmem()] * 2,
        out_specs=[vmem()] * targets,
        compiler_params=pltpu.CompilerParams(vmem_limit_bytes=20 * MIB),
        cost_estimate=pl.CostEstimate(flops=1000, bytes_accessed=1000, transcendentals=0),
        name="output",
    )(rows, w_out)


def frequency_kernel(out):
    head_dim = out.shape[1]
    lane = lax.broadcasted_iota(jnp.int32, out.shape, 1)
    exponents = (lane % (head_dim // 2)).astype(jnp.float32) * (2.0 / head_dim)
    out[...] = jnp.exp(-math.log(THETA) * exponents)


def frequencies(head_dim, microseconds):
    return pl.pallas_call(
        frequency_kernel,
        out_shape=jax.ShapeDtypeStruct((8, head_dim), jnp.float32),
        out_specs=vmem(),
        compiler_params=pltpu.CompilerParams(vmem_limit_bytes=2 * MIB),
        cost_estimate=pl.CostEstimate(
            flops=int(microseconds * 1.15e9), bytes_accessed=1 << 16, transcendentals=0
        ),
        name="frequencies",
    )()


def tables_kernel(lengths, frequency, limits, cosine, sine):
    row_count, head_dim = limits.shape
    lane = lax.broadcasted_iota(jnp.int32, (1, head_dim), 1)
    for r in range(row_count):
        position = jnp.full((1, head_dim), lengths[r], jnp.int32)
        angle = position.astype(jnp.float32) * frequency[:1]
        turn = jnp.sin(angle)
        limits[r : r + 1, :] = position
        cosine[r : r + 1, :] = jnp.cos(angle)
        sine[r : r + 1, :] = jnp.where(lane < head_dim // 2, -turn, turn)


def tables_of(lengths, frequency):
    shape = (lengths.shape[0], frequency.shape[1])
    return pl.pallas_call(
        tables_kernel,
        out_shape=[jax.ShapeDtypeStruct(shape, t) for t in (jnp.int32, jnp.float32, jnp.float32)],
        in_specs=[smem(), vmem()],
        out_specs=[vmem()] * 3,
        compiler_params=pltpu.CompilerParams(vmem_limit_bytes=2 * MIB),
        cost_estimate=pl.CostEstimate(flops=1000, bytes_accessed=1000, transcendentals=0),
        name="tables",
    )(lengths, frequency)


def body(
    hidden,
    lengths,
    w_query,
    key_weight,
    value_weight,
    w_out,
    key_cache,
    cached_values,
    *,
    wide,
    narrow,
):
    row_count, kv, _, head_dim = key_cache.shape
    heads = w_query.shape[1] // head_dim
    rows_out = hidden.shape[0]
    blocks = rows_out // row_count

    def target(owner):
        first, rest = lax.div(owner, blocks), lax.rem(owner, blocks)
        if direct(narrow):
            first = lax.bitwise_xor(lax.axis_index("narrow"), first)
        return first * blocks + rest

    def place(t):
        return target(peer(lax.axis_index("wide"), t, wide))

    frequency, hidden = lax.optimization_barrier((frequencies(head_dim, 100), hidden))
    hidden_pieces = gather_pieces(hidden, "narrow", narrow)
    parts = project(
        lambda t: place(t) * row_count,
        hidden_pieces,
        load(w_query, key_weight, value_weight),
        key_weight,
        value_weight,
        w_query,
        wide,
        row_count,
        heads,
        kv,
    )
    *parts, frequency = relay(relay([*parts, frequency], 30), 100)
    tables = tables_of(lengths, frequency)
    parts = scatter_pieces(parts, "wide", wide)
    context = attend(tables, key_cache, cached_values, parts, heads, kv)
    context_pieces = gather_pieces(context, "wide", wide)
    rows = arrange(place, context_pieces, row_count, heads)
    sums = output(rows, w_out, rows_out, narrow)
    sums = scatter_pieces(sums, "narrow", narrow)
    result = sums[0]
    for s in sums[1:]:
        result = result + s
    return result.astype(jnp.bfloat16)


def solution(mesh):
    in_specs = (
        P(("groups", "narrow"), "wide"),
        P(("groups", "wide")),
        P("wide", "narrow"),
        P("wide", "narrow"),
        P("wide", "narrow"),
        P("narrow", "wide"),
        P(("groups", "wide"), "narrow", None, None),
        P(("groups", "wide"), "narrow", None, None),
    )
    return jax.shard_map(
        functools.partial(body, wide=mesh.shape["wide"], narrow=mesh.shape["narrow"]),
        mesh=mesh,
        in_specs=in_specs,
        out_specs=P(("groups", "narrow"), "wide"),
        check_vma=False,
    )
```

```python
import functools
import math

import jax
import jax.numpy as jnp
from jax import lax
from jax.experimental import pallas as pl
from jax.experimental.pallas import tpu as pltpu
from jax.sharding import PartitionSpec as P

MIB = 1 << 20
LANES = 128
THETA = 500000.0
HEAD_SHARE = 4
LOADS = 4
SLOTS = 6
CUTS = 2
DIRECT_PEERS = 8


def xor_pairs(count, step):
    return [(i, i ^ step) for i in range(count)]


def direct(count):
    return count <= DIRECT_PEERS and count & (count - 1) == 0


def gather_pieces(piece, axis, count):
    if direct(count):
        return [piece] + [lax.ppermute(piece, axis, xor_pairs(count, t)) for t in range(1, count)]
    whole = lax.all_gather(piece, axis, axis=0, tiled=False)
    return [whole[t] for t in range(count)]


def scatter_pieces(pieces, axis, count):
    if direct(count):
        arrived = [
            lax.ppermute(pieces[t], axis, xor_pairs(count, t)) for t in reversed(range(1, count))
        ]
        return [pieces[0]] + arrived
    return [lax.psum_scatter(jnp.stack(pieces), axis, scatter_dimension=0, tiled=False)]


def peer(me, t, count):
    return lax.bitwise_xor(me, t) if direct(count) else jnp.int32(t)


def smem():
    return pl.BlockSpec(memory_space=pltpu.SMEM)


def vmem():
    return pl.BlockSpec(memory_space=pltpu.VMEM)


def head_depth(w_query):
    return w_query.shape[0] // HEAD_SHARE


def load_kernel(w_query, key_weight, value_weight, head, sems):
    del key_weight, value_weight
    depth = head.shape[0] // LOADS
    copies = [
        pltpu.make_async_copy(
            w_query.at[pl.ds(i * depth, depth)], head.at[pl.ds(i * depth, depth)], sems.at[i]
        )
        for i in range(LOADS)
    ]
    for copy in copies:
        copy.start()
    for copy in copies:
        copy.wait()


def load(w_query, key_weight, value_weight):
    shape = (head_depth(w_query), w_query.shape[1])
    return pl.pallas_call(
        load_kernel,
        out_shape=jax.ShapeDtypeStruct(shape, w_query.dtype),
        in_specs=[pl.BlockSpec(memory_space=pltpu.HBM), vmem(), vmem()],
        out_specs=vmem(),
        scratch_shapes=[pltpu.SemaphoreType.DMA((LOADS,))],
        compiler_params=pltpu.CompilerParams(vmem_limit_bytes=2 * MIB),
        cost_estimate=pl.CostEstimate(
            flops=1000, bytes_accessed=2 * math.prod(shape), transcendentals=0
        ),
        name="load",
    )(pltpu.with_memory_space_constraint(w_query, pltpu.HBM), key_weight, value_weight)


def project_kernel(
    head, key_weight, value_weight, w_query, *refs, pieces, heads, kv, stride, place, depth, slots
):
    inputs, refs = refs[:pieces], refs[pieces:]
    outs, (rows, total, laid, held, sems) = refs[:-5], refs[-5:]
    count, width = rows.shape
    done = head.shape[0]
    cut = held.shape[2]
    cuts = w_query.shape[1] // cut
    chunks = (width - done) // depth * cuts
    group = min(8, count)

    def copy(i):
        start, first = done + i // cuts * depth, i % cuts * cut
        return pltpu.make_async_copy(
            w_query.at[pl.ds(start, depth), pl.ds(first, cut)],
            held.at[i % slots],
            sems.at[i % slots],
        )

    def lay(sums, first):
        for base in range(0, count, group):
            for h in range(sums.shape[1] // LANES):
                laid[pl.ds(base * stride + first + h, group, stride=stride), :] = sums[
                    base : base + group, h * LANES : (h + 1) * LANES
                ]

    for i in range(min(slots, chunks)):
        copy(i).start()
    rows[...] = jnp.concatenate([p[...].astype(jnp.float32) for p in inputs], 0).astype(
        jnp.bfloat16
    )
    half = width // 2
    for i, w in enumerate((key_weight, value_weight)):
        lay(
            jnp.dot(rows[:, :half], w[:half], preferred_element_type=jnp.float32)
            + jnp.dot(rows[:, half:], w[half:], preferred_element_type=jnp.float32),
            heads + i * kv,
        )
    total[...] = jnp.dot(rows[:, :done], head[...], preferred_element_type=jnp.float32)
    for i in range(chunks):
        copy(i).wait()
        start, first = done + i // cuts * depth, i % cuts * cut
        total[:, first : first + cut] += jnp.dot(
            rows[:, start : start + depth], held[i % slots], preferred_element_type=jnp.float32
        )
        if i + slots < chunks:
            copy(i + slots).start()
        if i + cuts >= chunks:
            lay(total[:, first : first + cut], first // LANES)
    for t, out in enumerate(outs):
        out[...] = laid[pl.ds(pl.multiple_of(place(t) * stride, 8), out.shape[0]), :]


def project(
    place, hidden_pieces, head, key_weight, value_weight, w_query, targets, row_count, heads, kv
):
    stride = -(-(heads + 2 * kv) // 8) * 8
    width, columns = w_query.shape
    count = sum(p.shape[0] for p in hidden_pieces)
    depth = math.gcd(256, width - head.shape[0])
    scratch = SLOTS * depth * (columns // CUTS) * 2 + count * (columns + stride * LANES) * 4
    return pl.pallas_call(
        functools.partial(
            project_kernel,
            pieces=len(hidden_pieces),
            heads=heads,
            kv=kv,
            stride=stride,
            place=place,
            depth=depth,
            slots=SLOTS,
        ),
        out_shape=[jax.ShapeDtypeStruct((row_count * stride, LANES), jnp.float32)] * targets,
        in_specs=[vmem()] * 3
        + [pl.BlockSpec(memory_space=pltpu.HBM)]
        + [vmem()] * len(hidden_pieces),
        out_specs=[vmem()] * targets,
        scratch_shapes=[
            pltpu.VMEM((count, width), jnp.bfloat16),
            pltpu.VMEM((count, columns), jnp.float32),
            pltpu.VMEM((count * stride, LANES), jnp.float32),
            pltpu.VMEM((SLOTS, depth, columns // CUTS), jnp.bfloat16),
            pltpu.SemaphoreType.DMA((SLOTS,)),
        ],
        compiler_params=pltpu.CompilerParams(vmem_limit_bytes=(scratch // MIB + 1 + count // 16) * MIB),
        cost_estimate=pl.CostEstimate(flops=1000, bytes_accessed=1000, transcendentals=0),
        name="project",
    )(
        head,
        key_weight,
        value_weight,
        pltpu.with_memory_space_constraint(w_query, pltpu.HBM),
        *hidden_pieces,
    )


def relay_kernel(*refs):
    half = len(refs) // 2
    for source, target in zip(refs[:half], refs[half:], strict=True):
        target[...] = source[...]


def relay(arrays, microseconds):
    return pl.pallas_call(
        relay_kernel,
        out_shape=[jax.ShapeDtypeStruct(a.shape, a.dtype) for a in arrays],
        in_specs=[vmem()] * len(arrays),
        out_specs=[vmem()] * len(arrays),
        compiler_params=pltpu.CompilerParams(vmem_limit_bytes=2 * MIB),
        cost_estimate=pl.CostEstimate(
            flops=int(microseconds * 1.15e9), bytes_accessed=1 << 16, transcendentals=0
        ),
        name="relay",
    )(*arrays)


def attend_kernel(limits, cosine, sine, key_cache, cached_values, *refs, heads, kv, stride):
    parts, out = refs[:-1], refs[-1]
    row_count, _, slots, head_dim = key_cache.shape
    per = heads // kv
    scale = head_dim ** (-0.5)
    half = head_dim // 2
    position = lax.broadcasted_iota(jnp.int32, (per, slots), 1)
    pairs = [(r, g) for r in range(row_count) for g in range(kv)]
    queries, self_scores, values_new, scores = {}, {}, {}, {}
    for r in range(row_count):
        span = slice(r * stride, (r + 1) * stride)
        summed = parts[0][span, :]
        for p in parts[1:]:
            summed = summed + p[span, :]
        cos_row, sin_row = cosine[r : r + 1, :], sine[r : r + 1, :]
        turned = jnp.concatenate([summed[:, half:], summed[:, :half]], 1)
        rotated = (summed * cos_row + turned * sin_row).astype(jnp.bfloat16)
        for g in range(kv):
            queries[r, g] = rotated[g * per : (g + 1) * per]
            key_new = rotated[heads + g : heads + g + 1].astype(jnp.float32)
            self_scores[r, g] = (
                jnp.sum(queries[r, g].astype(jnp.float32) * key_new, -1, keepdims=True) * scale
            )
            values_new[r, g] = summed[heads + kv + g : heads + kv + g + 1].astype(jnp.bfloat16)
    for r, g in pairs:
        scores[r, g] = lax.dot_general(
            queries[r, g],
            key_cache[r, g],
            (((1,), (1,)), ((), ())),
            preferred_element_type=jnp.float32,
        )
    weights, self_weights, denominators = {}, {}, {}
    for r, g in pairs:
        masked = jnp.where(position < limits[r : r + 1, :1], scores[r, g] * scale, -jnp.inf)
        highest = jnp.maximum(jnp.max(masked, -1, keepdims=True), self_scores[r, g])
        raised = jnp.exp(masked - highest)
        self_weight = jnp.exp(self_scores[r, g] - highest)
        denominators[r, g] = jnp.sum(raised, -1, keepdims=True) + self_weight
        weights[r, g] = raised.astype(jnp.bfloat16)
        self_weights[r, g] = self_weight.astype(jnp.bfloat16).astype(jnp.float32)
    for r, g in pairs:
        mixed = jnp.dot(
            weights[r, g], cached_values[r, g], preferred_element_type=jnp.float32
        ) + self_weights[r, g] * values_new[r, g].astype(jnp.float32)
        start = r * heads + g * per
        out[start : start + per, :] = (mixed / denominators[r, g]).astype(jnp.bfloat16)


def attend(tables, key_cache, cached_values, parts, heads, kv):
    row_count = key_cache.shape[0]
    stride = parts[0].shape[0] // row_count
    return pl.pallas_call(
        functools.partial(attend_kernel, heads=heads, kv=kv, stride=stride),
        out_shape=jax.ShapeDtypeStruct((row_count * heads, LANES), jnp.bfloat16),
        in_specs=[vmem()] * (5 + len(parts)),
        out_specs=vmem(),
        compiler_params=pltpu.CompilerParams(vmem_limit_bytes=6 * MIB),
        cost_estimate=pl.CostEstimate(flops=1000, bytes_accessed=1000, transcendentals=0),
        name="attend",
    )(
        *tables,
        key_cache,
        cached_values,
        *parts,
    )


def arrange_kernel(*refs, pieces, heads, place):
    inputs, (rows, laid, total) = refs[:pieces][::-1], refs[pieces:]
    for t, piece in enumerate(inputs):
        laid[place(t)] = piece[...].astype(jnp.float32)
    flat = laid.reshape(laid.shape[0] * laid.shape[1], LANES)
    count = rows.shape[0]
    group = min(8, count)
    for base in range(0, count, group):
        for h in range(heads):
            total[base : base + group, h * LANES : (h + 1) * LANES] = flat[
                pl.ds(base * heads + h, group, stride=heads), :
            ]
    rows[...] = total[...].astype(jnp.bfloat16)


def arrange(place, pieces, row_count, heads):
    count = row_count * len(pieces)
    return pl.pallas_call(
        functools.partial(arrange_kernel, pieces=len(pieces), heads=heads, place=place),
        out_shape=jax.ShapeDtypeStruct((count, heads * LANES), jnp.bfloat16),
        in_specs=[vmem()] * len(pieces),
        out_specs=vmem(),
        scratch_shapes=[
            pltpu.VMEM((len(pieces), row_count * heads, LANES), jnp.float32),
            pltpu.VMEM((count, heads * LANES), jnp.float32),
        ],
        compiler_params=pltpu.CompilerParams(vmem_limit_bytes=6 * MIB),
        cost_estimate=pl.CostEstimate(flops=1000, bytes_accessed=1000, transcendentals=0),
        name="arrange",
    )(*pieces[::-1])


def output_kernel(rows, w_out, *outs, rows_out):
    columns = w_out.shape[1]
    step = min(1024, columns)
    for j in range(0, columns, step):
        sums = jnp.dot(rows[...], w_out[:, j : j + step], preferred_element_type=jnp.float32)
        for s, out in enumerate(outs):
            out[:, j : j + step] = sums[s * rows_out : (s + 1) * rows_out, :]


def output(rows, w_out, rows_out, targets):
    columns = w_out.shape[1]
    return pl.pallas_call(
        functools.partial(output_kernel, rows_out=rows_out),
        out_shape=[jax.ShapeDtypeStruct((rows_out, columns), jnp.float32)] * targets,
        in_specs=[vmem()] * 2,
        out_specs=[vmem()] * targets,
        compiler_params=pltpu.CompilerParams(vmem_limit_bytes=20 * MIB),
        cost_estimate=pl.CostEstimate(flops=1000, bytes_accessed=1000, transcendentals=0),
        name="output",
    )(rows, w_out)


def frequency_kernel(out):
    head_dim = out.shape[1]
    lane = lax.broadcasted_iota(jnp.int32, out.shape, 1)
    exponents = (lane % (head_dim // 2)).astype(jnp.float32) * (2.0 / head_dim)
    out[...] = jnp.exp(-math.log(THETA) * exponents)


def frequencies(head_dim, microseconds):
    return pl.pallas_call(
        frequency_kernel,
        out_shape=jax.ShapeDtypeStruct((8, head_dim), jnp.float32),
        out_specs=vmem(),
        compiler_params=pltpu.CompilerParams(vmem_limit_bytes=2 * MIB),
        cost_estimate=pl.CostEstimate(
            flops=int(microseconds * 1.15e9), bytes_accessed=1 << 16, transcendentals=0
        ),
        name="frequencies",
    )()


def tables_kernel(lengths, frequency, limits, cosine, sine):
    row_count, head_dim = limits.shape
    lane = lax.broadcasted_iota(jnp.int32, (1, head_dim), 1)
    for r in range(row_count):
        position = jnp.full((1, head_dim), lengths[r], jnp.int32)
        angle = position.astype(jnp.float32) * frequency[:1]
        turn = jnp.sin(angle)
        limits[r : r + 1, :] = position
        cosine[r : r + 1, :] = jnp.cos(angle)
        sine[r : r + 1, :] = jnp.where(lane < head_dim // 2, -turn, turn)


def tables_of(lengths, frequency):
    shape = (lengths.shape[0], frequency.shape[1])
    return pl.pallas_call(
        tables_kernel,
        out_shape=[jax.ShapeDtypeStruct(shape, t) for t in (jnp.int32, jnp.float32, jnp.float32)],
        in_specs=[smem(), vmem()],
        out_specs=[vmem()] * 3,
        compiler_params=pltpu.CompilerParams(vmem_limit_bytes=2 * MIB),
        cost_estimate=pl.CostEstimate(flops=1000, bytes_accessed=1000, transcendentals=0),
        name="tables",
    )(lengths, frequency)


def body(
    hidden,
    lengths,
    w_query,
    key_weight,
    value_weight,
    w_out,
    key_cache,
    cached_values,
    *,
    wide,
    narrow,
):
    row_count, kv, _, head_dim = key_cache.shape
    heads = w_query.shape[1] // head_dim
    rows_out = hidden.shape[0]
    blocks = rows_out // row_count

    def target(owner):
        first, rest = lax.div(owner, blocks), lax.rem(owner, blocks)
        if direct(narrow):
            first = lax.bitwise_xor(lax.axis_index("narrow"), first)
        return first * blocks + rest

    def place(t):
        return target(peer(lax.axis_index("wide"), t, wide))

    frequency = frequencies(head_dim, 100)
    hidden_pieces = gather_pieces(hidden, "narrow", narrow)
    parts = project(
        lambda t: place(t) * row_count,
        hidden_pieces,
        load(w_query, key_weight, value_weight),
        key_weight,
        value_weight,
        w_query,
        wide,
        row_count,
        heads,
        kv,
    )
    *parts, frequency = relay(relay([*parts, frequency], 30), 100)
    tables = tables_of(lengths, frequency)
    parts = scatter_pieces(parts, "wide", wide)
    context = attend(tables, key_cache, cached_values, parts, heads, kv)
    context_pieces = gather_pieces(context, "wide", wide)
    rows = arrange(place, context_pieces, row_count, heads)
    sums = output(rows, w_out, rows_out, narrow)
    sums = scatter_pieces(sums, "narrow", narrow)
    result = sums[0]
    for s in sums[-1:] + sums[1:-1]:
        result = result + s
    return result.astype(jnp.bfloat16)


def solution(mesh):
    in_specs = (
        P(("groups", "narrow"), "wide"),
        P(("groups", "wide")),
        P("wide", "narrow"),
        P("wide", "narrow"),
        P("wide", "narrow"),
        P("narrow", "wide"),
        P(("groups", "wide"), "narrow", None, None),
        P(("groups", "wide"), "narrow", None, None),
    )
    return jax.shard_map(
        functools.partial(body, wide=mesh.shape["wide"], narrow=mesh.shape["narrow"]),
        mesh=mesh,
        in_specs=in_specs,
        out_specs=P(("groups", "narrow"), "wide"),
        check_vma=False,
    )
```

```python
import functools
import math

import jax
import jax.numpy as jnp
from jax import lax
from jax.experimental import pallas as pl
from jax.experimental.pallas import tpu as pltpu
from jax.sharding import PartitionSpec as P

MIB = 1 << 20
LANES = 128
THETA = 500000.0
HEAD_SHARE = 4
LOADS = 4
SLOTS = 6
CUTS = 2
DIRECT_PEERS = 8


def xor_pairs(count, step):
    return [(i, i ^ step) for i in range(count)]


def direct(count):
    return count <= DIRECT_PEERS and count & (count - 1) == 0


def gather_pieces(piece, axis, count):
    if direct(count):
        return [piece] + [lax.ppermute(piece, axis, xor_pairs(count, t)) for t in range(1, count)]
    whole = lax.all_gather(piece, axis, axis=0, tiled=False)
    return [whole[t] for t in range(count)]


def scatter_pieces(pieces, axis, count):
    if direct(count):
        arrived = [
            lax.ppermute(pieces[t], axis, xor_pairs(count, t)) for t in reversed(range(1, count))
        ]
        return [pieces[0]] + arrived
    return [lax.psum_scatter(jnp.stack(pieces), axis, scatter_dimension=0, tiled=False)]


def peer(me, t, count):
    return lax.bitwise_xor(me, t) if direct(count) else jnp.int32(t)


def smem():
    return pl.BlockSpec(memory_space=pltpu.SMEM)


def vmem():
    return pl.BlockSpec(memory_space=pltpu.VMEM)


def head_depth(w_query):
    return w_query.shape[0] // HEAD_SHARE


def load_kernel(w_query, key_weight, value_weight, head, sems):
    del key_weight, value_weight
    depth = head.shape[0] // LOADS
    copies = [
        pltpu.make_async_copy(
            w_query.at[pl.ds(i * depth, depth)], head.at[pl.ds(i * depth, depth)], sems.at[i]
        )
        for i in range(LOADS)
    ]
    for copy in copies:
        copy.start()
    for copy in copies:
        copy.wait()


def load(w_query, key_weight, value_weight):
    shape = (head_depth(w_query), w_query.shape[1])
    return pl.pallas_call(
        load_kernel,
        out_shape=jax.ShapeDtypeStruct(shape, w_query.dtype),
        in_specs=[pl.BlockSpec(memory_space=pltpu.HBM), vmem(), vmem()],
        out_specs=vmem(),
        scratch_shapes=[pltpu.SemaphoreType.DMA((LOADS,))],
        compiler_params=pltpu.CompilerParams(vmem_limit_bytes=2 * MIB),
        cost_estimate=pl.CostEstimate(
            flops=1000, bytes_accessed=2 * math.prod(shape), transcendentals=0
        ),
        name="load",
    )(pltpu.with_memory_space_constraint(w_query, pltpu.HBM), key_weight, value_weight)


def project_kernel(
    head, key_weight, value_weight, w_query, *refs, pieces, heads, kv, stride, place, depth, slots
):
    inputs, refs = refs[:pieces], refs[pieces:]
    outs, (rows, total, laid, held, sems) = refs[:-5], refs[-5:]
    count, width = rows.shape
    done = head.shape[0]
    cut = held.shape[2]
    cuts = w_query.shape[1] // cut
    chunks = (width - done) // depth * cuts
    group = min(8, count)

    def copy(i):
        start, first = done + i // cuts * depth, i % cuts * cut
        return pltpu.make_async_copy(
            w_query.at[pl.ds(start, depth), pl.ds(first, cut)],
            held.at[i % slots],
            sems.at[i % slots],
        )

    def lay(sums, first):
        for base in range(0, count, group):
            for h in range(sums.shape[1] // LANES):
                laid[pl.ds(base * stride + first + h, group, stride=stride), :] = sums[
                    base : base + group, h * LANES : (h + 1) * LANES
                ]

    for i in range(min(slots, chunks)):
        copy(i).start()
    rows[...] = jnp.concatenate([p[...].astype(jnp.float32) for p in inputs], 0).astype(
        jnp.bfloat16
    )
    half = width // 2
    for i, w in enumerate((key_weight, value_weight)):
        lay(
            jnp.dot(rows[:, :half], w[:half], preferred_element_type=jnp.float32)
            + jnp.dot(rows[:, half:], w[half:], preferred_element_type=jnp.float32),
            heads + i * kv,
        )
    total[...] = jnp.dot(rows[:, :done], head[...], preferred_element_type=jnp.float32)
    for i in range(chunks):
        copy(i).wait()
        start, first = done + i // cuts * depth, i % cuts * cut
        total[:, first : first + cut] += jnp.dot(
            rows[:, start : start + depth], held[i % slots], preferred_element_type=jnp.float32
        )
        if i + slots < chunks:
            copy(i + slots).start()
        if i + cuts >= chunks:
            lay(total[:, first : first + cut], first // LANES)
    for t, out in enumerate(outs):
        out[...] = laid[pl.ds(pl.multiple_of(place(t) * stride, 8), out.shape[0]), :]


def project(
    place, hidden_pieces, head, key_weight, value_weight, w_query, targets, row_count, heads, kv
):
    stride = -(-(heads + 2 * kv) // 8) * 8
    width, columns = w_query.shape
    count = sum(p.shape[0] for p in hidden_pieces)
    depth = math.gcd(256, width - head.shape[0])
    scratch = SLOTS * depth * (columns // CUTS) * 2 + count * (columns + stride * LANES) * 4
    return pl.pallas_call(
        functools.partial(
            project_kernel,
            pieces=len(hidden_pieces),
            heads=heads,
            kv=kv,
            stride=stride,
            place=place,
            depth=depth,
            slots=SLOTS,
        ),
        out_shape=[jax.ShapeDtypeStruct((row_count * stride, LANES), jnp.float32)] * targets,
        in_specs=[vmem()] * 3
        + [pl.BlockSpec(memory_space=pltpu.HBM)]
        + [vmem()] * len(hidden_pieces),
        out_specs=[vmem()] * targets,
        scratch_shapes=[
            pltpu.VMEM((count, width), jnp.bfloat16),
            pltpu.VMEM((count, columns), jnp.float32),
            pltpu.VMEM(((count + 1) * stride, LANES), jnp.float32),
            pltpu.VMEM((SLOTS, depth, columns // CUTS), jnp.bfloat16),
            pltpu.SemaphoreType.DMA((SLOTS,)),
        ],
        compiler_params=pltpu.CompilerParams(vmem_limit_bytes=(scratch // MIB + 1 + count // 16) * MIB),
        cost_estimate=pl.CostEstimate(flops=1000, bytes_accessed=1000, transcendentals=0),
        name="project",
    )(
        head,
        key_weight,
        value_weight,
        pltpu.with_memory_space_constraint(w_query, pltpu.HBM),
        *hidden_pieces,
    )


def relay_kernel(*refs):
    half = len(refs) // 2
    for source, target in zip(refs[:half], refs[half:], strict=True):
        target[...] = source[...]


def relay(arrays, microseconds):
    return pl.pallas_call(
        relay_kernel,
        out_shape=[jax.ShapeDtypeStruct(a.shape, a.dtype) for a in arrays],
        in_specs=[vmem()] * len(arrays),
        out_specs=[vmem()] * len(arrays),
        compiler_params=pltpu.CompilerParams(vmem_limit_bytes=2 * MIB),
        cost_estimate=pl.CostEstimate(
            flops=int(microseconds * 1.15e9), bytes_accessed=1 << 16, transcendentals=0
        ),
        name="relay",
    )(*arrays)


def attend_kernel(limits, cosine, sine, key_cache, cached_values, *refs, heads, kv, stride):
    parts, out = refs[:-1], refs[-1]
    row_count, _, slots, head_dim = key_cache.shape
    per = heads // kv
    scale = head_dim ** (-0.5)
    half = head_dim // 2
    position = lax.broadcasted_iota(jnp.int32, (per, slots), 1)
    pairs = [(r, g) for r in range(row_count) for g in range(kv)]
    queries, self_scores, values_new, scores = {}, {}, {}, {}
    for r in range(row_count):
        span = slice(r * stride, (r + 1) * stride)
        summed = parts[0][span, :]
        for p in parts[1:]:
            summed = summed + p[span, :]
        cos_row, sin_row = cosine[r : r + 1, :], sine[r : r + 1, :]
        turned = jnp.concatenate([summed[:, half:], summed[:, :half]], 1)
        rotated = (summed * cos_row + turned * sin_row).astype(jnp.bfloat16)
        for g in range(kv):
            queries[r, g] = rotated[g * per : (g + 1) * per]
            key_new = rotated[heads + g : heads + g + 1].astype(jnp.float32)
            self_scores[r, g] = (
                jnp.sum(queries[r, g].astype(jnp.float32) * key_new, -1, keepdims=True) * scale
            )
            values_new[r, g] = summed[heads + kv + g : heads + kv + g + 1].astype(jnp.bfloat16)
    for r, g in pairs:
        scores[r, g] = lax.dot_general(
            queries[r, g],
            key_cache[r, g],
            (((1,), (1,)), ((), ())),
            preferred_element_type=jnp.float32,
        )
    weights, self_weights, denominators = {}, {}, {}
    for r, g in pairs:
        masked = jnp.where(position < limits[r : r + 1, :1], scores[r, g] * scale, -jnp.inf)
        highest = jnp.maximum(jnp.max(masked, -1, keepdims=True), self_scores[r, g])
        raised = jnp.exp(masked - highest)
        self_weight = jnp.exp(self_scores[r, g] - highest)
        denominators[r, g] = jnp.sum(raised, -1, keepdims=True) + self_weight
        weights[r, g] = raised.astype(jnp.bfloat16)
        self_weights[r, g] = self_weight.astype(jnp.bfloat16).astype(jnp.float32)
    for r, g in pairs:
        mixed = jnp.dot(
            weights[r, g], cached_values[r, g], preferred_element_type=jnp.float32
        ) + self_weights[r, g] * values_new[r, g].astype(jnp.float32)
        start = r * heads + g * per
        out[start : start + per, :] = (mixed / denominators[r, g]).astype(jnp.bfloat16)


def attend(tables, key_cache, cached_values, parts, heads, kv):
    row_count = key_cache.shape[0]
    stride = parts[0].shape[0] // row_count
    return pl.pallas_call(
        functools.partial(attend_kernel, heads=heads, kv=kv, stride=stride),
        out_shape=jax.ShapeDtypeStruct((row_count * heads, LANES), jnp.bfloat16),
        in_specs=[vmem()] * (5 + len(parts)),
        out_specs=vmem(),
        compiler_params=pltpu.CompilerParams(vmem_limit_bytes=6 * MIB),
        cost_estimate=pl.CostEstimate(flops=1000, bytes_accessed=1000, transcendentals=0),
        name="attend",
    )(
        *tables,
        key_cache,
        cached_values,
        *parts,
    )


def arrange_kernel(*refs, pieces, heads, place):
    inputs, (rows, laid, total) = refs[:pieces][::-1], refs[pieces:]
    for t, piece in enumerate(inputs):
        laid[place(t)] = piece[...].astype(jnp.float32)
    flat = laid.reshape(laid.shape[0] * laid.shape[1], LANES)
    count = rows.shape[0]
    group = min(8, count)
    for base in range(0, count, group):
        for h in range(heads):
            total[base : base + group, h * LANES : (h + 1) * LANES] = flat[
                pl.ds(base * heads + h, group, stride=heads), :
            ]
    rows[...] = total[...].astype(jnp.bfloat16)


def arrange(place, pieces, row_count, heads):
    count = row_count * len(pieces)
    return pl.pallas_call(
        functools.partial(arrange_kernel, pieces=len(pieces), heads=heads, place=place),
        out_shape=jax.ShapeDtypeStruct((count, heads * LANES), jnp.bfloat16),
        in_specs=[vmem()] * len(pieces),
        out_specs=vmem(),
        scratch_shapes=[
            pltpu.VMEM((len(pieces) + 1, row_count * heads, LANES), jnp.float32),
            pltpu.VMEM((count, heads * LANES), jnp.float32),
        ],
        compiler_params=pltpu.CompilerParams(vmem_limit_bytes=6 * MIB),
        cost_estimate=pl.CostEstimate(flops=1000, bytes_accessed=1000, transcendentals=0),
        name="arrange",
    )(*pieces[::-1])


def output_kernel(rows, w_out, *outs, rows_out):
    columns = w_out.shape[1]
    step = min(1024, columns)
    for j in range(0, columns, step):
        sums = jnp.dot(rows[...], w_out[:, j : j + step], preferred_element_type=jnp.float32)
        for s, out in enumerate(outs):
            out[:, j : j + step] = sums[s * rows_out : (s + 1) * rows_out, :]


def output(rows, w_out, rows_out, targets):
    columns = w_out.shape[1]
    return pl.pallas_call(
        functools.partial(output_kernel, rows_out=rows_out),
        out_shape=[jax.ShapeDtypeStruct((rows_out, columns), jnp.float32)] * targets,
        in_specs=[vmem()] * 2,
        out_specs=[vmem()] * targets,
        compiler_params=pltpu.CompilerParams(vmem_limit_bytes=20 * MIB),
        cost_estimate=pl.CostEstimate(flops=1000, bytes_accessed=1000, transcendentals=0),
        name="output",
    )(rows, w_out)


def frequency_kernel(out):
    head_dim = out.shape[1]
    lane = lax.broadcasted_iota(jnp.int32, out.shape, 1)
    exponents = (lane % (head_dim // 2)).astype(jnp.float32) * (2.0 / head_dim)
    out[...] = jnp.exp(-math.log(THETA) * exponents)


def frequencies(head_dim, microseconds):
    return pl.pallas_call(
        frequency_kernel,
        out_shape=jax.ShapeDtypeStruct((8, head_dim), jnp.float32),
        out_specs=vmem(),
        compiler_params=pltpu.CompilerParams(vmem_limit_bytes=2 * MIB),
        cost_estimate=pl.CostEstimate(
            flops=int(microseconds * 1.15e9), bytes_accessed=1 << 16, transcendentals=0
        ),
        name="frequencies",
    )()


def tables_kernel(lengths, frequency, limits, cosine, sine):
    row_count, head_dim = limits.shape
    lane = lax.broadcasted_iota(jnp.int32, (1, head_dim), 1)
    for r in range(row_count):
        position = jnp.full((1, head_dim), lengths[r], jnp.int32)
        angle = position.astype(jnp.float32) * frequency[:1]
        turn = jnp.sin(angle)
        limits[r : r + 1, :] = position
        cosine[r : r + 1, :] = jnp.cos(angle)
        sine[r : r + 1, :] = jnp.where(lane < head_dim // 2, -turn, turn)


def tables_of(lengths, frequency):
    shape = (lengths.shape[0], frequency.shape[1])
    return pl.pallas_call(
        tables_kernel,
        out_shape=[jax.ShapeDtypeStruct(shape, t) for t in (jnp.int32, jnp.float32, jnp.float32)],
        in_specs=[smem(), vmem()],
        out_specs=[vmem()] * 3,
        compiler_params=pltpu.CompilerParams(vmem_limit_bytes=2 * MIB),
        cost_estimate=pl.CostEstimate(flops=1000, bytes_accessed=1000, transcendentals=0),
        name="tables",
    )(lengths, frequency)


def body(
    hidden,
    lengths,
    w_query,
    key_weight,
    value_weight,
    w_out,
    key_cache,
    cached_values,
    *,
    wide,
    narrow,
):
    row_count, kv, _, head_dim = key_cache.shape
    heads = w_query.shape[1] // head_dim
    rows_out = hidden.shape[0]
    blocks = rows_out // row_count

    def target(owner):
        first, rest = lax.div(owner, blocks), lax.rem(owner, blocks)
        if direct(narrow):
            first = lax.bitwise_xor(lax.axis_index("narrow"), first)
        return first * blocks + rest

    def place(t):
        return target(peer(lax.axis_index("wide"), t, wide))

    frequency = frequencies(head_dim, 100)
    hidden_pieces = gather_pieces(hidden, "narrow", narrow)
    parts = project(
        lambda t: place(t) * row_count,
        hidden_pieces,
        load(w_query, key_weight, value_weight),
        key_weight,
        value_weight,
        w_query,
        wide,
        row_count,
        heads,
        kv,
    )
    *parts, frequency = relay(relay([*parts, frequency], 30), 100)
    tables = tables_of(lengths, frequency)
    parts = scatter_pieces(parts, "wide", wide)
    context = attend(tables, key_cache, cached_values, parts, heads, kv)
    context_pieces = gather_pieces(context, "wide", wide)
    rows = arrange(place, context_pieces, row_count, heads)
    sums = output(rows, w_out, rows_out, narrow)
    sums = scatter_pieces(sums, "narrow", narrow)
    result = sums[0]
    for s in sums[-1:] + sums[1:-1]:
        result = result + s
    return result.astype(jnp.bfloat16)


def solution(mesh):
    in_specs = (
        P(("groups", "narrow"), "wide"),
        P(("groups", "wide")),
        P("wide", "narrow"),
        P("wide", "narrow"),
        P("wide", "narrow"),
        P("narrow", "wide"),
        P(("groups", "wide"), "narrow", None, None),
        P(("groups", "wide"), "narrow", None, None),
    )
    return jax.shard_map(
        functools.partial(body, wide=mesh.shape["wide"], narrow=mesh.shape["narrow"]),
        mesh=mesh,
        in_specs=in_specs,
        out_specs=P(("groups", "narrow"), "wide"),
        check_vma=False,
    )
```

```python
import functools
import math

import jax
import jax.numpy as jnp
from jax import lax
from jax.experimental import pallas as pl
from jax.experimental.pallas import tpu as pltpu
from jax.sharding import PartitionSpec as P

MIB = 1 << 20
LANES = 128
THETA = 500000.0
HEAD_SHARE = 4
LOADS = 4
SLOTS = 6
CUTS = 2
DIRECT_PEERS = 8


def xor_pairs(count, step):
    return [(i, i ^ step) for i in range(count)]


def direct(count):
    return count <= DIRECT_PEERS and count & (count - 1) == 0


def gather_pieces(piece, axis, count):
    if direct(count):
        return [piece] + [lax.ppermute(piece, axis, xor_pairs(count, t)) for t in range(1, count)]
    whole = lax.all_gather(piece, axis, axis=0, tiled=False)
    return [whole[t] for t in range(count)]


def scatter_pieces(pieces, axis, count):
    if direct(count):
        arrived = [
            lax.ppermute(pieces[t], axis, xor_pairs(count, t)) for t in reversed(range(1, count))
        ]
        return [pieces[0]] + arrived
    return [lax.psum_scatter(jnp.stack(pieces), axis, scatter_dimension=0, tiled=False)]


def peer(me, t, count):
    return lax.bitwise_xor(me, t) if direct(count) else jnp.int32(t)


def smem():
    return pl.BlockSpec(memory_space=pltpu.SMEM)


def vmem():
    return pl.BlockSpec(memory_space=pltpu.VMEM)


def head_depth(w_query):
    return w_query.shape[0] // HEAD_SHARE


def load_kernel(w_query, key_weight, value_weight, head, sems):
    del key_weight, value_weight
    depth = head.shape[0] // LOADS
    copies = [
        pltpu.make_async_copy(
            w_query.at[pl.ds(i * depth, depth)], head.at[pl.ds(i * depth, depth)], sems.at[i]
        )
        for i in range(LOADS)
    ]
    for copy in copies:
        copy.start()
    for copy in copies:
        copy.wait()


def load(w_query, key_weight, value_weight):
    shape = (head_depth(w_query), w_query.shape[1])
    return pl.pallas_call(
        load_kernel,
        out_shape=jax.ShapeDtypeStruct(shape, w_query.dtype),
        in_specs=[pl.BlockSpec(memory_space=pltpu.HBM), vmem(), vmem()],
        out_specs=vmem(),
        scratch_shapes=[pltpu.SemaphoreType.DMA((LOADS,))],
        compiler_params=pltpu.CompilerParams(vmem_limit_bytes=2 * MIB),
        cost_estimate=pl.CostEstimate(
            flops=1000, bytes_accessed=2 * math.prod(shape), transcendentals=0
        ),
        name="load",
    )(pltpu.with_memory_space_constraint(w_query, pltpu.HBM), key_weight, value_weight)


def project_kernel(
    head, key_weight, value_weight, w_query, *refs, pieces, heads, kv, stride, place, depth, slots
):
    inputs, refs = refs[:pieces], refs[pieces:]
    outs, (rows, total, laid, held, sems) = refs[:-5], refs[-5:]
    count, width = rows.shape
    done = head.shape[0]
    cut = held.shape[2]
    cuts = w_query.shape[1] // cut
    chunks = (width - done) // depth * cuts
    group = min(8, count)

    def copy(i):
        start, first = done + i // cuts * depth, i % cuts * cut
        return pltpu.make_async_copy(
            w_query.at[pl.ds(start, depth), pl.ds(first, cut)],
            held.at[i % slots],
            sems.at[i % slots],
        )

    def lay(sums, first):
        for base in range(0, count, group):
            for h in range(sums.shape[1] // LANES):
                laid[pl.ds(base * stride + first + h, group, stride=stride), :] = sums[
                    base : base + group, h * LANES : (h + 1) * LANES
                ]

    for i in range(min(slots, chunks)):
        copy(i).start()
    rows[...] = jnp.concatenate([p[...].astype(jnp.float32) for p in inputs], 0).astype(
        jnp.bfloat16
    )
    half = width // 2
    for i, w in enumerate((key_weight, value_weight)):
        lay(
            jnp.dot(rows[:, :half], w[:half], preferred_element_type=jnp.float32)
            + jnp.dot(rows[:, half:], w[half:], preferred_element_type=jnp.float32),
            heads + i * kv,
        )
    total[...] = jnp.dot(rows[:, :done], head[...], preferred_element_type=jnp.float32)
    for i in range(chunks):
        copy(i).wait()
        start, first = done + i // cuts * depth, i % cuts * cut
        total[:, first : first + cut] += jnp.dot(
            rows[:, start : start + depth], held[i % slots], preferred_element_type=jnp.float32
        )
        if i + slots < chunks:
            copy(i + slots).start()
        if i + cuts >= chunks:
            lay(total[:, first : first + cut], first // LANES)
    for t, out in enumerate(outs):
        out[...] = laid[pl.ds(pl.multiple_of(place(t) * stride, 8), out.shape[0]), :]


def project(
    place, hidden_pieces, head, key_weight, value_weight, w_query, targets, row_count, heads, kv
):
    stride = -(-(heads + 2 * kv) // 8) * 8
    width, columns = w_query.shape
    count = sum(p.shape[0] for p in hidden_pieces)
    depth = math.gcd(256, width - head.shape[0])
    scratch = SLOTS * depth * (columns // CUTS) * 2 + count * (columns + stride * LANES) * 4
    return pl.pallas_call(
        functools.partial(
            project_kernel,
            pieces=len(hidden_pieces),
            heads=heads,
            kv=kv,
            stride=stride,
            place=place,
            depth=depth,
            slots=SLOTS,
        ),
        out_shape=[jax.ShapeDtypeStruct((row_count * stride, LANES), jnp.float32)] * targets,
        in_specs=[vmem()] * 3
        + [pl.BlockSpec(memory_space=pltpu.HBM)]
        + [vmem()] * len(hidden_pieces),
        out_specs=[vmem()] * targets,
        scratch_shapes=[
            pltpu.VMEM((count, width), jnp.bfloat16),
            pltpu.VMEM((count, columns), jnp.float32),
            pltpu.VMEM(((count + 1) * stride, LANES), jnp.float32),
            pltpu.VMEM((SLOTS, depth, columns // CUTS), jnp.bfloat16),
            pltpu.SemaphoreType.DMA((SLOTS,)),
        ],
        compiler_params=pltpu.CompilerParams(vmem_limit_bytes=(scratch // MIB + 1 + count // 16) * MIB),
        cost_estimate=pl.CostEstimate(flops=1000, bytes_accessed=1000, transcendentals=0),
        name="project",
    )(
        head,
        key_weight,
        value_weight,
        pltpu.with_memory_space_constraint(w_query, pltpu.HBM),
        *hidden_pieces,
    )


def relay_kernel(*refs):
    half = len(refs) // 2
    for source, target in zip(refs[:half], refs[half:], strict=True):
        target[...] = source[...]


def relay(arrays, microseconds):
    return pl.pallas_call(
        relay_kernel,
        out_shape=[jax.ShapeDtypeStruct(a.shape, a.dtype) for a in arrays],
        in_specs=[vmem()] * len(arrays),
        out_specs=[vmem()] * len(arrays),
        compiler_params=pltpu.CompilerParams(vmem_limit_bytes=2 * MIB),
        cost_estimate=pl.CostEstimate(
            flops=int(microseconds * 1.15e9), bytes_accessed=1 << 16, transcendentals=0
        ),
        name="relay",
    )(*arrays)


def attend_kernel(limits, cosine, sine, key_cache, cached_values, *refs, heads, kv, stride):
    parts, out = refs[:-1], refs[-1]
    row_count, _, slots, head_dim = key_cache.shape
    per = heads // kv
    scale = head_dim ** (-0.5)
    half = head_dim // 2
    position = lax.broadcasted_iota(jnp.int32, (per, slots), 1)
    pairs = [(r, g) for r in range(row_count) for g in range(kv)]
    queries, self_scores, values_new, scores = {}, {}, {}, {}
    for r in range(row_count):
        span = slice(r * stride, (r + 1) * stride)
        summed = parts[0][span, :]
        for p in parts[1:]:
            summed = summed + p[span, :]
        cos_row, sin_row = cosine[r : r + 1, :], sine[r : r + 1, :]
        turned = jnp.concatenate([summed[:, half:], summed[:, :half]], 1)
        rotated = (summed * cos_row + turned * sin_row).astype(jnp.bfloat16)
        for g in range(kv):
            queries[r, g] = rotated[g * per : (g + 1) * per]
            key_new = rotated[heads + g : heads + g + 1].astype(jnp.float32)
            self_scores[r, g] = (
                jnp.sum(queries[r, g].astype(jnp.float32) * key_new, -1, keepdims=True) * scale
            )
            values_new[r, g] = summed[heads + kv + g : heads + kv + g + 1].astype(jnp.bfloat16)
    for r, g in pairs:
        scores[r, g] = lax.dot_general(
            queries[r, g],
            key_cache[r, g],
            (((1,), (1,)), ((), ())),
            preferred_element_type=jnp.float32,
        )
    weights, self_weights, denominators = {}, {}, {}
    for r, g in pairs:
        masked = jnp.where(position < limits[r : r + 1, :1], scores[r, g] * scale, -jnp.inf)
        highest = jnp.maximum(jnp.max(masked, -1, keepdims=True), self_scores[r, g])
        raised = jnp.exp(masked - highest)
        self_weight = jnp.exp(self_scores[r, g] - highest)
        denominators[r, g] = jnp.sum(raised, -1, keepdims=True) + self_weight
        weights[r, g] = raised.astype(jnp.bfloat16)
        self_weights[r, g] = self_weight.astype(jnp.bfloat16).astype(jnp.float32)
    for r, g in pairs:
        mixed = jnp.dot(
            weights[r, g], cached_values[r, g], preferred_element_type=jnp.float32
        ) + self_weights[r, g] * values_new[r, g].astype(jnp.float32)
        start = r * heads + g * per
        out[start : start + per, :] = (mixed / denominators[r, g]).astype(jnp.bfloat16)


def attend(tables, key_cache, cached_values, parts, heads, kv):
    row_count = key_cache.shape[0]
    stride = parts[0].shape[0] // row_count
    return pl.pallas_call(
        functools.partial(attend_kernel, heads=heads, kv=kv, stride=stride),
        out_shape=jax.ShapeDtypeStruct((row_count * heads, LANES), jnp.bfloat16),
        in_specs=[vmem()] * (5 + len(parts)),
        out_specs=vmem(),
        compiler_params=pltpu.CompilerParams(vmem_limit_bytes=6 * MIB),
        cost_estimate=pl.CostEstimate(flops=1000, bytes_accessed=1000, transcendentals=0),
        name="attend",
    )(
        *tables,
        key_cache,
        cached_values,
        *parts,
    )


def arrange_kernel(*refs, pieces, heads, place):
    inputs, (rows, laid, total) = refs[:pieces][::-1], refs[pieces:]
    for t, piece in enumerate(inputs):
        laid[place(t)] = piece[...].astype(jnp.float32)
    flat = laid.reshape(laid.shape[0] * laid.shape[1], LANES)
    count = rows.shape[0]
    group = min(8, count)
    for base in range(0, count, group):
        for h in range(heads):
            total[base : base + group, h * LANES : (h + 1) * LANES] = flat[
                pl.ds(base * heads + h, group, stride=heads), :
            ]
    rows[...] = total[...].astype(jnp.bfloat16)


def arrange(place, pieces, row_count, heads):
    count = row_count * len(pieces)
    return pl.pallas_call(
        functools.partial(arrange_kernel, pieces=len(pieces), heads=heads, place=place),
        out_shape=jax.ShapeDtypeStruct((count, heads * LANES), jnp.bfloat16),
        in_specs=[vmem()] * len(pieces),
        out_specs=vmem(),
        scratch_shapes=[
            pltpu.VMEM((len(pieces) + 1, row_count * heads, LANES), jnp.float32),
            pltpu.VMEM((count, heads * LANES), jnp.float32),
        ],
        compiler_params=pltpu.CompilerParams(vmem_limit_bytes=6 * MIB),
        cost_estimate=pl.CostEstimate(flops=1000, bytes_accessed=1000, transcendentals=0),
        name="arrange",
    )(*pieces[::-1])


def output_kernel(rows, w_out, *outs, rows_out):
    columns = w_out.shape[1]
    step = min(1024, columns)
    for j in range(0, columns, step):
        sums = jnp.dot(rows[...], w_out[:, j : j + step], preferred_element_type=jnp.float32)
        for s, out in enumerate(outs):
            out[:, j : j + step] = sums[s * rows_out : (s + 1) * rows_out, :]


def output(rows, w_out, rows_out, targets):
    columns = w_out.shape[1]
    return pl.pallas_call(
        functools.partial(output_kernel, rows_out=rows_out),
        out_shape=[jax.ShapeDtypeStruct((rows_out, columns), jnp.float32)] * targets,
        in_specs=[vmem()] * 2,
        out_specs=[vmem()] * targets,
        compiler_params=pltpu.CompilerParams(vmem_limit_bytes=20 * MIB),
        cost_estimate=pl.CostEstimate(flops=1000, bytes_accessed=1000, transcendentals=0),
        name="output",
    )(rows, w_out)


def frequency_kernel(out):
    head_dim = out.shape[1]
    lane = lax.broadcasted_iota(jnp.int32, out.shape, 1)
    exponents = (lane % (head_dim // 2)).astype(jnp.float32) * (2.0 / head_dim)
    out[...] = jnp.exp(-math.log(THETA) * exponents)


def frequencies(head_dim, microseconds):
    return pl.pallas_call(
        frequency_kernel,
        out_shape=jax.ShapeDtypeStruct((8, head_dim), jnp.float32),
        out_specs=vmem(),
        compiler_params=pltpu.CompilerParams(vmem_limit_bytes=2 * MIB),
        cost_estimate=pl.CostEstimate(
            flops=int(microseconds * 1.15e9), bytes_accessed=1 << 16, transcendentals=0
        ),
        name="frequencies",
    )()


def tables_kernel(lengths, frequency, limits, cosine, sine):
    row_count, head_dim = limits.shape
    lane = lax.broadcasted_iota(jnp.int32, (1, head_dim), 1)
    for r in range(row_count):
        position = jnp.full((1, head_dim), lengths[r], jnp.int32)
        angle = position.astype(jnp.float32) * frequency[:1]
        turn = jnp.sin(angle)
        limits[r : r + 1, :] = position
        cosine[r : r + 1, :] = jnp.cos(angle)
        sine[r : r + 1, :] = jnp.where(lane < head_dim // 2, -turn, turn)


def tables_of(lengths, frequency):
    shape = (lengths.shape[0], frequency.shape[1])
    return pl.pallas_call(
        tables_kernel,
        out_shape=[jax.ShapeDtypeStruct(shape, t) for t in (jnp.int32, jnp.float32, jnp.float32)],
        in_specs=[smem(), vmem()],
        out_specs=[vmem()] * 3,
        compiler_params=pltpu.CompilerParams(vmem_limit_bytes=2 * MIB),
        cost_estimate=pl.CostEstimate(flops=1000, bytes_accessed=1000, transcendentals=0),
        name="tables",
    )(lengths, frequency)


def body(
    hidden,
    lengths,
    w_query,
    key_weight,
    value_weight,
    w_out,
    key_cache,
    cached_values,
    *,
    wide,
    narrow,
):
    row_count, kv, _, head_dim = key_cache.shape
    heads = w_query.shape[1] // head_dim
    rows_out = hidden.shape[0]
    blocks = rows_out // row_count

    def target(owner):
        first, rest = lax.div(owner, blocks), lax.rem(owner, blocks)
        if direct(narrow):
            first = lax.bitwise_xor(lax.axis_index("narrow"), first)
        return first * blocks + rest

    def place(t):
        return target(peer(lax.axis_index("wide"), t, wide))

    frequency = frequencies(head_dim, 100)
    hidden_pieces = gather_pieces(hidden, "narrow", narrow)
    parts = project(
        lambda t: place(t) * row_count,
        hidden_pieces,
        load(w_query, key_weight, value_weight),
        key_weight,
        value_weight,
        w_query,
        wide,
        row_count,
        heads,
        kv,
    )
    *parts, frequency = relay(relay([*parts, frequency], 30), 100)
    tables = tables_of(lengths, frequency)
    parts = scatter_pieces(parts, "wide", wide)
    context = attend(tables, key_cache, cached_values, parts, heads, kv)
    context_pieces = gather_pieces(context, "wide", wide)
    rows = arrange(place, context_pieces, row_count, heads)
    sums = output(rows, w_out, rows_out, narrow)
    sums = scatter_pieces(sums, "narrow", narrow)
    result, *others = sums
    for s in others[-1:] + others[:-1]:
        result = result + s
    return result.astype(jnp.bfloat16)


def solution(mesh):
    in_specs = (
        P(("groups", "narrow"), "wide"),
        P(("groups", "wide")),
        P("wide", "narrow"),
        P("wide", "narrow"),
        P("wide", "narrow"),
        P("narrow", "wide"),
        P(("groups", "wide"), "narrow", None, None),
        P(("groups", "wide"), "narrow", None, None),
    )
    return jax.shard_map(
        functools.partial(body, wide=mesh.shape["wide"], narrow=mesh.shape["narrow"]),
        mesh=mesh,
        in_specs=in_specs,
        out_specs=P(("groups", "narrow"), "wide"),
        check_vma=False,
    )
```
